256 devices in a mesh: seq: 64 (over z, y, core), grp: 4 (over x).
Axes of the slice: x: 4, y: 4, z: 8, core: 2. Of those that a mesh axis runs over, the one named last changes fastest.
Arguments:
- queries: bfloat16 [65536, 1024], P(('seq', 'grp')), may hold values from -5 to 5
- key_rows: bfloat16 [65536, 128], P(('seq', 'grp')), may hold values from -5 to 5
- value_rows: bfloat16 [65536, 128], P(('seq', 'grp')), may hold values from -6 to 6
- out_grad: bfloat16 [65536, 1024], P(('seq', 'grp')), may hold values from -6 to 6
- segment: int32 [65536], P(('seq', 'grp')), may hold values from 0 to 84, never falling along the last dimension, each value on 1 to 1536 neighbouring positions
Outputs:
- attended: bfloat16 [65536, 1024], P(('seq', 'grp'))
- query_grad: bfloat16 [65536, 1024], P(('seq', 'grp'))
- key_grad: float32 [65536, 128], P(('seq', 'grp'))
- value_grad: float32 [65536, 128], P(('seq', 'grp'))
The draws below stay inside these ranges and needn't reach their ends.
Inputs may be any that keep to these rules, and one draw needn't show every extreme that they name: `segment`: segment numbers start at 0 and never fall along the sequence; every document holds 1 to 1536 tokens, and one holds exactly 1536.
All inputs are finite; a program needn't handle non-finite values.
Results may differ from the reference program's by a relative error of at most 0.019.
Values may be sent and summed in bfloat16 or wider, within the bound.
No kernel may reach another device: no remote copies, remote signals or barrier semaphores. Data moves between devices by JAX's collectives and lax.ppermute only.
A program may use at most 64 MiB of HBM per device.

```python
import math
import jax
import jax.numpy as jnp
import numpy as np
from jax import lax

HEADS = 8
HD = 128
TOK_DEV = 256
MAXDOC = 1536
TOKENS = 65536
SEGMENTS = 85


def pair_draw(key):
    base = jax.random.fold_in(key, 7)
    streams = jax.random.split(base, 2)
    query_draw = jnp.clip(jax.random.normal(streams[0], (TOKENS, HEADS * HD), jnp.float32), -5.0, 5.0)
    key_draw = jnp.clip(jax.random.normal(streams[1], (TOKENS, HD), jnp.float32), -5.0, 5.0)
    return (query_draw, key_draw)


def draw_queries(key, part):
    return pair_draw(key)[0].astype(jnp.bfloat16)


def draw_key_rows(key, part):
    return pair_draw(key)[1].astype(jnp.bfloat16)


def steps_of(own_key, shape, pieces, smallest, high):
    factor_of = 1.0
    for axis_at, parts in pieces:
        draws = jax.random.uniform(jax.random.fold_in(jax.random.fold_in(own_key, 6), axis_at), (parts,), jnp.float32, smallest / len(pieces), high / len(pieces))
        factor_of = factor_of * jnp.repeat(jnp.exp(draws), shape[axis_at] // parts).reshape((-1,) + (1,) * (len(shape) - 1 - axis_at))
    return factor_of


def length_profile(count, total, bound, slope):
    loads = [(1 << 20) // math.isqrt(standing ** slope) + 1 for standing in range(2, count + 1)]
    rest, counts = total - bound - (count - 1), [1] * (count - 1)
    while rest > 0:
        free = [i for i in range(count - 1) if counts[i] < bound]
        whole, budget = sum([loads[i] for i in free]), rest
        for i in free:
            addition = min(bound - counts[i], max(1, budget * loads[i] // whole), rest)
            counts[i] = counts[i] + addition
            rest = rest - addition
    return np.array([bound] + counts)


def ragged(own_key, count, total, limit, slope):
    if count == 2:
        one = jax.random.randint(own_key, (), max(1, total - limit), min(limit, total - 1) + 1)
        return jnp.stack([one, total - one])
    tallies = jnp.asarray(length_profile(count, total, limit, slope), jnp.int32)
    couples = (count - 1) // 2
    donor, sink = tallies[1:1 + 2 * couples:2], tallies[2:2 + 2 * couples:2]
    room = jnp.minimum(donor - 1, limit - sink)
    shifted = jax.random.randint(jax.random.fold_in(own_key, 1), (couples,), 0, 1 << 20) % (room + 1)
    tallies = tallies.at[1:1 + 2 * couples:2].set(donor - shifted).at[2:2 + 2 * couples:2].set(sink + shifted)
    return tallies[jax.random.permutation(jax.random.fold_in(own_key, 2), count)]


def normal_values(key, extent, scale, most, cuts=(), kind=jnp.bfloat16):
    result = scale * jax.random.normal(key, extent, jnp.float32)
    if cuts:
        result = result * steps_of(key, extent, cuts, -0.22, 0.18)
    return jnp.clip(result, -most, most).astype(kind)


def setup_inputs(seed: int = 0) -> dict:
    seeds = jax.random.split(jax.random.key(seed), 6)
    queries = draw_queries(jax.random.fold_in(seeds[5], 71), 0)
    key_rows = draw_key_rows(jax.random.fold_in(seeds[5], 71), 0)
    value_rows = normal_values(seeds[2], (TOKENS, HD), 1.0, 6.0, ((0, 256),))
    out_grad = normal_values(seeds[3], (TOKENS, HEADS * HD), 1.0, 6.0, ((0, 256),))
    segment = jnp.searchsorted(jnp.cumsum(ragged(seeds[4], SEGMENTS, TOKENS, MAXDOC, 1)), jnp.arange(TOKENS), side="right").astype(jnp.int32)
    return dict(queries=queries, key_rows=key_rows, value_rows=value_rows, out_grad=out_grad, segment=segment)


def reference(queries, key_rows, value_rows, out_grad, segment):
    score_scale = HD ** -0.5
    block_rows = 512 if TOKENS % 512 == 0 else TOK_DEV
    block_count = TOKENS // block_rows
    window = MAXDOC + block_rows
    keys_padded = jnp.concatenate([jnp.zeros((MAXDOC, HD), key_rows.dtype), key_rows], axis=0)
    values_padded = jnp.concatenate([jnp.zeros((MAXDOC, HD), value_rows.dtype), value_rows], axis=0)
    segment_padded = jnp.concatenate([jnp.full((MAXDOC,), -1, jnp.int32), segment.astype(jnp.int32)], axis=0)

    def one_block(running, index):
        key_total, value_total = running
        start = (index * block_rows).astype(jnp.int32)
        query_block = lax.dynamic_slice_in_dim(queries, start, block_rows, 0).astype(jnp.float32).reshape(block_rows, HEADS, HD)
        grad_block = lax.dynamic_slice_in_dim(out_grad, start, block_rows, 0).astype(jnp.float32).reshape(block_rows, HEADS, HD)
        query_seg = lax.dynamic_slice_in_dim(segment.astype(jnp.int32), start, block_rows, 0)
        key_window = lax.dynamic_slice_in_dim(keys_padded, start, window, 0).astype(jnp.float32)
        value_window = lax.dynamic_slice_in_dim(values_padded, start, window, 0).astype(jnp.float32)
        key_seg = lax.dynamic_slice_in_dim(segment_padded, start, window, 0)
        query_pos = start + jnp.arange(block_rows, dtype=jnp.int32)
        key_pos = start - MAXDOC + jnp.arange(window, dtype=jnp.int32)
        visible = (key_seg[None, :] == query_seg[:, None]) & (key_pos[None, :] <= query_pos[:, None])
        visible = visible[:, None, :]
        scores = jnp.einsum("thd,kd->thk", query_block, key_window) * score_scale
        row_max = jnp.max(jnp.where(visible, scores, -1e30), axis=-1)
        row_sum = jnp.sum(jnp.where(visible, jnp.exp(scores - row_max[..., None]), 0.0), axis=-1)
        log_total = row_max + jnp.log(row_sum)
        prob = jnp.where(visible, jnp.exp(scores - log_total[..., None]), 0.0)
        weight = prob.astype(jnp.bfloat16)
        attended = jnp.einsum("thk,kd->thd", weight.astype(jnp.float32), value_window).astype(jnp.bfloat16)
        row_dot = jnp.sum(grad_block * attended.astype(jnp.float32), axis=-1)
        dprob = jnp.einsum("thd,kd->thk", grad_block, value_window)
        dscore = (score_scale * prob * (dprob - row_dot[..., None])).astype(jnp.bfloat16)
        query_grad = jnp.einsum("thk,kd->thd", dscore.astype(jnp.float32), key_window).astype(jnp.bfloat16)
        key_part = jnp.einsum("thk,thd->kd", dscore.astype(jnp.float32), query_block)
        value_part = jnp.einsum("thk,thd->kd", weight.astype(jnp.float32), grad_block)
        key_total = lax.dynamic_update_slice_in_dim(key_total, lax.dynamic_slice_in_dim(key_total, start, window, 0) + key_part, start, 0)
        value_total = lax.dynamic_update_slice_in_dim(value_total, lax.dynamic_slice_in_dim(value_total, start, window, 0) + value_part, start, 0)
        return (key_total, value_total), (attended.reshape(block_rows, HEADS * HD), query_grad.reshape(block_rows, HEADS * HD))

    start_totals = (jnp.zeros((MAXDOC + TOKENS, HD), jnp.float32), jnp.zeros((MAXDOC + TOKENS, HD), jnp.float32))
    totals, outputs = lax.scan(one_block, start_totals, jnp.arange(block_count, dtype=jnp.int32))
    attended = outputs[0].reshape(TOKENS, HEADS * HD)
    query_grad = outputs[1].reshape(TOKENS, HEADS * HD)
    return attended, query_grad, totals[0][MAXDOC:], totals[1][MAXDOC:]
```

```python
import functools
import math

import jax
import jax.numpy as jnp
from jax import lax
from jax.experimental import pallas as pl
from jax.experimental.pallas import tpu as pltpu
from jax.sharding import PartitionSpec as P

AXES = ("seq", "grp")
BACK = 6
HIDE = -1e30


def wrapped(value, steps):
    count = lax.axis_size(AXES)
    return lax.ppermute(value, AXES, [(i, (i + steps) % count) for i in range(count)])


def nt(a, b):
    return lax.dot_general(a, b, (((1,), (1,)), ((), ())), preferred_element_type=jnp.float32)


def nn(a, b):
    return lax.dot_general(a, b, (((1,), (0,)), ((), ())), preferred_element_type=jnp.float32)


def attention_kernel(
    heads,
    q_ref,
    g_ref,
    *refs,
):
    blocks = refs[: BACK + 1]
    o_ref, dq_ref, own_ref = refs[BACK + 1 : BACK + 4]
    parts = refs[BACK + 4 : 2 * BACK + 4]
    kt, vt, qs, gs, sc, ex, bias, dots = refs[2 * BACK + 4 :]
    tokens = q_ref.shape[0]
    width = q_ref.shape[1] // heads
    scale = width**-0.5
    scale2 = scale * math.log2(math.e)
    chunks = BACK + 1

    def rows(c):
        return slice(c * tokens, (c + 1) * tokens)

    own_seg = blocks[0][tokens : tokens + 8, :].astype(jnp.float32)
    row_seg = own_seg[0:1, :]
    key_seg = jnp.transpose(own_seg)[:, 0:1]
    key_at = lax.broadcasted_iota(jnp.int32, (tokens, tokens), 0)
    row_at = lax.broadcasted_iota(jnp.int32, (tokens, tokens), 1)
    bias[rows(0), :] = jnp.where((key_seg == row_seg) & (key_at <= row_at), 0.0, HIDE)
    first = row_seg[:, 0:1]
    for c in range(1, chunks):
        seg = blocks[c][tokens : tokens + 8, :].astype(jnp.float32)[0:1, :]
        count = jnp.sum(jnp.where(seg == first, 1.0, 0.0), axis=1, keepdims=True)
        shown = (key_at.astype(jnp.float32) >= tokens - count) & (row_seg == first)
        bias[rows(c), :] = jnp.where(shown, 0.0, HIDE)
    for c in range(chunks):
        kt[:, rows(c)] = jnp.transpose(blocks[c][0:tokens, 0:width])
        vt[:, rows(c)] = jnp.transpose(blocks[c][0:tokens, width : 2 * width])

    def forward(h, carry):
        lanes = pl.ds(pl.multiple_of(h * width, width), width)
        at = pl.ds(pl.multiple_of(h * tokens, tokens), tokens)
        q = q_ref[:, lanes]
        qs[at, :] = q
        top = jnp.full((1, tokens), HIDE, jnp.float32)
        for c in range(chunks):
            s = nt(blocks[c][0:tokens, 0:width], q) * scale2 + bias[rows(c), :]
            sc[rows(c), :] = s
            top = jnp.maximum(top, jnp.max(s, axis=0, keepdims=True))
        total = jnp.zeros((1, tokens), jnp.float32)
        for c in range(chunks):
            e = jnp.exp2(sc[rows(c), :] - top)
            total = total + jnp.sum(e, axis=0, keepdims=True)
            ex[rows(c), at] = e.astype(jnp.bfloat16)
        inv = 1.0 / total
        out = jnp.transpose(nn(vt[...], ex[:, at]) * inv)
        o_ref[:, lanes] = out.astype(o_ref.dtype)
        inv_rows = jnp.transpose(jnp.broadcast_to(inv, (8, tokens)))[:, 0:1]
        g = (g_ref[:, lanes].astype(jnp.float32) * inv_rows).astype(jnp.bfloat16)
        gs[at, :] = g
        prod = g.astype(jnp.float32) * out
        high = prod.astype(jnp.bfloat16)
        low = (prod - high.astype(jnp.float32)).astype(jnp.bfloat16)
        ones = jnp.ones((8, width), jnp.bfloat16)
        dots[:, at] = nt(ones, high) + nt(ones, low)
        return carry

    lax.fori_loop(0, heads, forward, 0)

    for c in range(chunks):
        part = own_ref if c == 0 else parts[c - 1]
        part[:, width : 2 * width] = nn(ex[rows(c), :], gs[...]).astype(part.dtype)

        def backward(h, carry, c=c):
            at = pl.ds(pl.multiple_of(h * tokens, tokens), tokens)
            d = nt(blocks[c][0:tokens, width : 2 * width], gs[at, :]) - dots[0:1, at]
            ex[rows(c), at] = (ex[rows(c), at].astype(jnp.float32) * d).astype(jnp.bfloat16)
            return carry

        lax.fori_loop(0, heads, backward, 0)
        part[:, 0:width] = (nn(ex[rows(c), :], qs[...]) * scale).astype(part.dtype)

    def query_step(h, carry):
        lanes = pl.ds(pl.multiple_of(h * width, width), width)
        at = pl.ds(pl.multiple_of(h * tokens, tokens), tokens)
        dq_t = nn(kt[...], ex[:, at]) * scale
        dq_ref[:, lanes] = jnp.transpose(dq_t).astype(dq_ref.dtype)
        return carry

    lax.fori_loop(0, heads, query_step, 0)


def attention(queries, out_grad, blocks):
    tokens = queries.shape[0]
    width = blocks[0].shape[1] // 2
    heads = queries.shape[1] // width
    keys = (BACK + 1) * tokens
    vmem = pl.BlockSpec(memory_space=pltpu.VMEM)
    return pl.pallas_call(
        functools.partial(attention_kernel, heads),
        out_shape=(
            jax.ShapeDtypeStruct(queries.shape, jnp.bfloat16),
            jax.ShapeDtypeStruct(queries.shape, jnp.bfloat16),
            jax.ShapeDtypeStruct((tokens, 2 * width), jnp.float32),
        )
        + (jax.ShapeDtypeStruct((tokens, 2 * width), jnp.bfloat16),) * BACK,
        in_specs=[vmem] * (BACK + 3),
        out_specs=(vmem,) * (BACK + 3),
        scratch_shapes=[
            pltpu.VMEM((width, keys), jnp.bfloat16),
            pltpu.VMEM((width, keys), jnp.bfloat16),
            pltpu.VMEM((heads * tokens, width), jnp.bfloat16),
            pltpu.VMEM((heads * tokens, width), jnp.bfloat16),
            pltpu.VMEM((keys, tokens), jnp.float32),
            pltpu.VMEM((keys, heads * tokens), jnp.bfloat16),
            pltpu.VMEM((keys, tokens), jnp.float32),
            pltpu.VMEM((8, heads * tokens), jnp.float32),
        ],
        compiler_params=pltpu.CompilerParams(vmem_limit_bytes=40 * 1024 * 1024),
        name="attention",
    )(queries, out_grad, *blocks)


def on_device(queries, key_rows, value_rows, out_grad, segment):
    tokens, width = key_rows.shape
    marks = jnp.broadcast_to(segment.astype(jnp.bfloat16)[None, :], (16, tokens))
    own = jnp.concatenate([jnp.concatenate([key_rows, value_rows], axis=1), marks], axis=0)
    blocks = [own] + [wrapped(own, d) for d in range(1, BACK + 1)]
    attended, query_grad, total, *parts = attention(queries, out_grad, blocks)
    for d in range(1, BACK + 1):
        total = total + wrapped(parts[d - 1], -d).astype(jnp.float32)
    return attended, query_grad, total[:, :width], total[:, width:]


def solution(mesh):
    spec = P(AXES, None)
    return jax.shard_map(
        on_device,
        mesh=mesh,
        in_specs=(spec, spec, spec, spec, P(AXES)),
        out_specs=(spec,) * 4,
        check_vma=False,
    )
```

```python
import functools
import math

import jax
import jax.numpy as jnp
from jax import lax
from jax.experimental import pallas as pl
from jax.experimental.pallas import tpu as pltpu
from jax.sharding import PartitionSpec as P

AXES = ("seq", "grp")
BACK = 6
SIZES = (2, 4, 6, 7)
HIDE = -1e30


def wrapped(value, steps):
    count = lax.axis_size(AXES)
    return lax.ppermute(value, AXES, [(i, (i + steps) % count) for i in range(count)])


def nt(a, b):
    return lax.dot_general(a, b, (((1,), (1,)), ((), ())), preferred_element_type=jnp.float32)


def nn(a, b):
    return lax.dot_general(a, b, (((1,), (0,)), ((), ())), preferred_element_type=jnp.float32)


def tn(a, b):
    return lax.dot_general(a, b, (((0,), (0,)), ((), ())), preferred_element_type=jnp.float32)


def attention_kernel(heads, q_ref, g_ref, *refs):
    blocks = refs[: BACK + 1]
    o_ref, dq_ref, own_ref = refs[BACK + 1 : BACK + 4]
    parts = refs[BACK + 4 : 2 * BACK + 4]
    ks, vs, bias, key_sum, value_sum = refs[2 * BACK + 4 : 2 * BACK + 9]
    rest = refs[2 * BACK + 9 :]
    sc, ex, ds, inv = rest[0:2], rest[2:4], rest[4:6], rest[6:8]
    tokens = q_ref.shape[0]
    width = q_ref.shape[1] // heads
    scale = width**-0.5
    scale2 = scale * math.log2(math.e)
    chunks = BACK + 1

    def rows(c):
        return slice(c * tokens, (c + 1) * tokens)

    own_seg = blocks[0][tokens : tokens + 8, :].astype(jnp.float32)
    row_seg = own_seg[0:1, :]
    key_seg = jnp.transpose(own_seg)[:, 0:1]
    key_at = lax.broadcasted_iota(jnp.int32, (tokens, tokens), 0)
    row_at = lax.broadcasted_iota(jnp.int32, (tokens, tokens), 1)
    bias[rows(0), :] = jnp.where((key_seg == row_seg) & (key_at <= row_at), 0.0, HIDE)
    first = row_seg[:, 0:1]
    reach = jnp.ones((1, 1), jnp.float32)
    for c in range(1, chunks):
        seg = blocks[c][tokens : tokens + 8, :].astype(jnp.float32)[0:1, :]
        count = jnp.sum(jnp.where(seg == first, 1.0, 0.0), axis=1, keepdims=True)
        reach = reach + jnp.where(count > 0, 1.0, 0.0)
        shown = (key_at.astype(jnp.float32) >= tokens - count) & (row_seg == first)
        bias[rows(c), :] = jnp.where(shown, 0.0, HIDE)
    for c in range(chunks):
        ks[rows(c), :] = blocks[c][0:tokens, 0:width]
        vs[rows(c), :] = blocks[c][0:tokens, width : 2 * width]
    needed = jnp.sum(reach).astype(jnp.int32)
    key_sum[...] = jnp.zeros_like(key_sum)
    value_sum[...] = jnp.zeros_like(value_sum)

    def lanes_of(h):
        return pl.ds(pl.multiple_of(h * width, width), width)

    def forward(h, slot, near):
        q = q_ref[:, lanes_of(h)]
        top = jnp.full((8, tokens), HIDE, jnp.float32)
        for c in range(near):
            s = nt(ks[rows(c), :], q) * scale2 + bias[rows(c), :]
            sc[slot][rows(c), :] = s
            top = jnp.maximum(top, jnp.max(s.reshape(-1, 8, tokens), axis=0))
        top = jnp.max(top, axis=0, keepdims=True)
        total = jnp.zeros((8, tokens), jnp.float32)
        for c in range(near):
            e = jnp.exp2(sc[slot][rows(c), :] - top)
            total = total + jnp.sum(e.reshape(-1, 8, tokens), axis=0)
            ex[slot][rows(c), :] = e.astype(jnp.bfloat16)
        total = jnp.sum(total, axis=0, keepdims=True)
        inv[slot][...] = jnp.broadcast_to(1.0 / total, (8, tokens))

    def backward(h, slot, near):
        lanes = lanes_of(h)
        seen = slice(0, near * tokens)
        q = q_ref[:, lanes]
        inv_rows = jnp.transpose(inv[slot][...])[:, 0:1]
        g = (g_ref[:, lanes].astype(jnp.float32) * inv_rows).astype(jnp.bfloat16)
        out = tn(ex[slot][seen, :], vs[seen, :]) * inv_rows
        o_ref[:, lanes] = out.astype(o_ref.dtype)
        value_sum[seen, :] += nn(ex[slot][seen, :], g)
        prod = g.astype(jnp.float32) * out
        high = prod.astype(jnp.bfloat16)
        low = (prod - high.astype(jnp.float32)).astype(jnp.bfloat16)
        ones = jnp.ones((8, width), jnp.bfloat16)
        dots = (nt(ones, high) + nt(ones, low))[0:1, :]
        for c in range(near):
            d = nt(vs[rows(c), :], g) - dots
            ds[slot][rows(c), :] = (ex[slot][rows(c), :].astype(jnp.float32) * d).astype(
                jnp.bfloat16
            )
        key_sum[seen, :] += nn(ds[slot][seen, :], q)
        dq_ref[:, lanes] = (tn(ds[slot][seen, :], ks[seen, :]) * scale).astype(dq_ref.dtype)

    below = 0
    for near in SIZES:

        @pl.when((needed > below) & (needed <= near))
        def _(near=near):
            def two(i, carry):
                forward(2 * i, 0, near)
                forward(2 * i + 1, 1, near)
                backward(2 * i, 0, near)
                backward(2 * i + 1, 1, near)
                return carry

            lax.fori_loop(0, heads // 2, two, 0)

        below = near

    for c in range(chunks):
        part = own_ref if c == 0 else parts[c - 1]
        part[:, 0:width] = (key_sum[rows(c), :] * scale).astype(part.dtype)
        part[:, width : 2 * width] = value_sum[rows(c), :].astype(part.dtype)


def attention(queries, out_grad, blocks):
    tokens = queries.shape[0]
    width = blocks[0].shape[1] // 2
    heads = queries.shape[1] // width
    keys = (BACK + 1) * tokens
    vmem = pl.BlockSpec(memory_space=pltpu.VMEM)
    return pl.pallas_call(
        functools.partial(attention_kernel, heads),
        out_shape=(
            jax.ShapeDtypeStruct(queries.shape, jnp.bfloat16),
            jax.ShapeDtypeStruct(queries.shape, jnp.bfloat16),
            jax.ShapeDtypeStruct((tokens, 2 * width), jnp.float32),
        )
        + (jax.ShapeDtypeStruct((tokens, 2 * width), jnp.bfloat16),) * BACK,
        in_specs=[vmem] * (BACK + 3),
        out_specs=(vmem,) * (BACK + 3),
        scratch_shapes=[
            pltpu.VMEM((keys, width), jnp.bfloat16),
            pltpu.VMEM((keys, width), jnp.bfloat16),
            pltpu.VMEM((keys, tokens), jnp.float32),
            pltpu.VMEM((keys, width), jnp.float32),
            pltpu.VMEM((keys, width), jnp.float32),
        ]
        + [pltpu.VMEM((keys, tokens), jnp.float32)] * 2
        + [pltpu.VMEM((keys, tokens), jnp.bfloat16)] * 4
        + [pltpu.VMEM((8, tokens), jnp.float32)] * 2,
        compiler_params=pltpu.CompilerParams(vmem_limit_bytes=40 * 1024 * 1024),
        name="attention",
    )(queries, out_grad, *blocks)


def on_device(queries, key_rows, value_rows, out_grad, segment):
    tokens, width = key_rows.shape
    marks = jnp.broadcast_to(segment.astype(jnp.bfloat16)[None, :], (16, tokens))
    own = jnp.concatenate([jnp.concatenate([key_rows, value_rows], axis=1), marks], axis=0)
    blocks = [own] + [wrapped(own, d) for d in range(1, BACK + 1)]
    attended, query_grad, total, *parts = attention(queries, out_grad, blocks)
    for d in range(1, BACK + 1):
        total = total + wrapped(parts[d - 1], -d).astype(jnp.float32)
    return attended, query_grad, total[:, :width], total[:, width:]


def solution(mesh):
    spec = P(AXES, None)
    return jax.shard_map(
        on_device,
        mesh=mesh,
        in_specs=(spec, spec, spec, spec, P(AXES)),
        out_specs=(spec,) * 4,
        check_vma=False,
    )
```

```python
import functools
import math

import jax
import jax.numpy as jnp
from jax import lax
from jax.experimental import pallas as pl
from jax.experimental.pallas import tpu as pltpu
from jax.sharding import PartitionSpec as P

AXES = ("seq", "grp")
NEAR = 3
FAR = 3
NEAR_SIZES = (2, 4)
FAR_SIZES = (0, 1, 3)
GROUP = 2
HIDE = -1e30


def wrapped(value, steps):
    count = lax.axis_size(AXES)
    return lax.ppermute(value, AXES, [(i, (i + steps) % count) for i in range(count)])


def dot(a, b, over_a, over_b):
    return lax.dot_general(
        a, b, (((over_a,), (over_b,)), ((), ())), preferred_element_type=jnp.float32
    )


def nt(a, b):
    return dot(a, b, 1, 1)


def nn(a, b):
    return dot(a, b, 1, 0)


def tn(a, b):
    return dot(a, b, 0, 0)


def rows(c, size):
    return slice(c * size, (c + 1) * size)


def at(h, size):
    return pl.ds(pl.multiple_of(h * size, size), size)


def marks_of(block, tokens):
    return block[tokens : tokens + 8, :].astype(jnp.float32)


def reached(seg_row, first):
    return jnp.sum(jnp.where(seg_row == first, 1.0, 0.0), axis=1, keepdims=True)


def bias_of(seg_row, row_seg, first, key_at):
    tokens = key_at.shape[0]
    count = reached(seg_row, first)
    shown = (key_at.astype(jnp.float32) >= tokens - count) & (row_seg == first)
    return jnp.where(shown, 0.0, HIDE), jnp.where(count > 0, 1.0, 0.0)


def for_heads(heads, needed, sizes, step):
    below = -1
    for size in sizes:

        @pl.when((needed > below) & (needed <= size))
        def _(size=size):
            def group(i, carry):
                step([i * GROUP + k for k in range(GROUP)], size)
                return carry

            lax.fori_loop(0, heads // GROUP, group, 0)

        below = size


def fold(op, x):
    return op(x.reshape(-1, 8, x.shape[1]), axis=0)


def near_forward(heads, q_ref, *refs):
    blocks = refs[: NEAR + 1]
    e_ref, o_ref, stat_ref, ks, vs, bias, *sc = refs[NEAR + 1 :]
    tokens = q_ref.shape[0]
    width = q_ref.shape[1] // heads
    scale2 = width**-0.5 * math.log2(math.e)
    own_seg = marks_of(blocks[0], tokens)
    row_seg = own_seg[0:1, :]
    key_seg = jnp.transpose(own_seg)[:, 0:1]
    key_at = lax.broadcasted_iota(jnp.int32, (tokens, tokens), 0)
    row_at = lax.broadcasted_iota(jnp.int32, (tokens, tokens), 1)
    bias[rows(0, tokens), :] = jnp.where((key_seg == row_seg) & (key_at <= row_at), 0.0, HIDE)
    first = row_seg[:, 0:1]
    reach = jnp.ones((1, 1), jnp.float32)
    for c in range(1, NEAR + 1):
        bias[rows(c, tokens), :], more = bias_of(
            marks_of(blocks[c], tokens)[0:1, :], row_seg, first, key_at
        )
        reach = reach + more
    for c in range(NEAR + 1):
        ks[rows(c, tokens), :] = blocks[c][0:tokens, 0:width]
        vs[rows(c, tokens), :] = blocks[c][0:tokens, width : 2 * width]

    def step(hs, size):
        for k, h in enumerate(hs):
            q = q_ref[:, at(h, width)]
            top = jnp.full((8, tokens), HIDE, jnp.float32)
            for c in range(size):
                r = rows(c, tokens)
                s = nt(ks[r, :], q) * scale2 + bias[r, :]
                sc[k][r, :] = s
                top = jnp.maximum(top, fold(jnp.max, s))
            top = jnp.max(top, axis=0, keepdims=True)
            total = jnp.zeros((8, tokens), jnp.float32)
            for c in range(size):
                r = rows(c, tokens)
                e = jnp.exp2(sc[k][r, :] - top)
                total = total + fold(jnp.sum, e)
                e_ref[r, at(h, tokens)] = e.astype(jnp.bfloat16)
            total = jnp.sum(total, axis=0, keepdims=True)
            stat_ref[0:8, at(h, tokens)] = jnp.broadcast_to(top, (8, tokens))
            stat_ref[8:16, at(h, tokens)] = jnp.broadcast_to(total, (8, tokens))
        seen = slice(0, size * tokens)
        for h in hs:
            o_ref[:, at(h, width)] = tn(e_ref[seen, at(h, tokens)], vs[seen, :])

    for_heads(heads, jnp.sum(reach).astype(jnp.int32), NEAR_SIZES, step)


def far_both(heads, q_ref, g_ref, near_out, stat_ref, own, far, *refs):
    o_ref, part, dq_ref, gn_ref, dots_ref, ks, vs, bias, sums, *slots = refs
    sc, ex, ds, gf, dt = (slots[i * GROUP : (i + 1) * GROUP] for i in range(5))
    tokens = q_ref.shape[0]
    width = q_ref.shape[1] // heads
    scale = width**-0.5
    scale2 = scale * math.log2(math.e)
    pitch = far.shape[0] // FAR
    row_seg = marks_of(own, tokens)[0:1, :]
    first = row_seg[:, 0:1]
    key_at = lax.broadcasted_iota(jnp.int32, (tokens, tokens), 0)
    reach = jnp.zeros((1, 1), jnp.float32)
    for c in range(FAR):
        seg = far[c * pitch + tokens : c * pitch + tokens + 8, :].astype(jnp.float32)[0:1, :]
        bias[rows(c, tokens), :], more = bias_of(seg, row_seg, first, key_at)
        reach = reach + more
        ks[rows(c, tokens), :] = far[c * pitch : c * pitch + tokens, 0:width]
        vs[rows(c, tokens), :] = far[c * pitch : c * pitch + tokens, width : 2 * width]
    sums[...] = jnp.zeros_like(sums)

    def step(hs, size):
        seen = slice(0, size * tokens)
        for k, h in enumerate(hs):
            q = q_ref[:, at(h, width)]
            lanes = at(h, tokens)
            old = stat_ref[0:1, lanes]
            top = jnp.broadcast_to(old, (8, tokens))
            for c in range(size):
                r = rows(c, tokens)
                s = nt(ks[r, :], q) * scale2 + bias[r, :]
                sc[k][r, :] = s
                top = jnp.maximum(top, fold(jnp.max, s))
            top = jnp.max(top, axis=0, keepdims=True)
            keep = jnp.exp2(old - top)
            total = jnp.zeros((8, tokens), jnp.float32)
            for c in range(size):
                r = rows(c, tokens)
                e = jnp.exp2(sc[k][r, :] - top)
                total = total + fold(jnp.sum, e)
                ex[k][r, :] = e.astype(jnp.bfloat16)
            total = jnp.sum(total, axis=0, keepdims=True) + stat_ref[8:9, lanes] * keep
            inv = 1.0 / total
            near = inv * keep
            both = jnp.concatenate(
                [jnp.broadcast_to(inv, (8, tokens)), jnp.broadcast_to(near, (8, tokens))], axis=0
            )
            cols = jnp.transpose(both)
            inv_rows, near_rows = cols[:, 0:1], cols[:, 8:9]
            g = g_ref[:, at(h, width)].astype(jnp.float32)
            gf[k][...] = (g * inv_rows).astype(jnp.bfloat16)
            gn_ref[lanes, :] = (g * near_rows).astype(jnp.bfloat16)
            out = near_out[:, at(h, width)] * near_rows
            if size:
                out = out + tn(ex[k][seen, :], vs[seen, :]) * inv_rows
            o_ref[:, at(h, width)] = out.astype(o_ref.dtype)
            prod = g * out
            high = prod.astype(jnp.bfloat16)
            low = (prod - high.astype(jnp.float32)).astype(jnp.bfloat16)
            ones = jnp.ones((8, width), jnp.bfloat16)
            dots = nt(ones, high) + nt(ones, low)
            dots_ref[:, lanes] = dots * near
            dt[k][...] = dots * inv
        for k, h in enumerate(hs):
            lanes = at(h, width)
            if not size:
                dq_ref[:, lanes] = jnp.zeros((tokens, width), jnp.float32)
                continue
            q = q_ref[:, lanes]
            g = gf[k][...]
            sums[seen, width : 2 * width] += nn(ex[k][seen, :], g)
            for c in range(size):
                r = rows(c, tokens)
                d = nt(vs[r, :], g) - dt[k][0:1, :]
                ds[k][r, :] = (ex[k][r, :].astype(jnp.float32) * d).astype(jnp.bfloat16)
            sums[seen, 0:width] += nn(ds[k][seen, :], q)
            dq_ref[:, lanes] = tn(ds[k][seen, :], ks[seen, :])

    for_heads(heads, jnp.sum(reach).astype(jnp.int32), FAR_SIZES, step)
    part[:, 0:width] = (sums[:, 0:width] * scale).astype(part.dtype)
    part[:, width : 2 * width] = sums[:, width : 2 * width].astype(part.dtype)


def near_backward(heads, q_ref, gn_ref, dots_ref, e_ref, far_dq, *refs):
    blocks = refs[: NEAR + 1]
    dq_ref, sums, ks, vs, *ds = refs[NEAR + 1 :]
    tokens = q_ref.shape[0]
    width = q_ref.shape[1] // heads
    scale = width**-0.5
    row_seg = marks_of(blocks[0], tokens)[0:1, :]
    reach = jnp.ones((1, 1), jnp.float32)
    for c in range(1, NEAR + 1):
        count = reached(marks_of(blocks[c], tokens)[0:1, :], row_seg[:, 0:1])
        reach = reach + jnp.where(count > 0, 1.0, 0.0)
    for c in range(NEAR + 1):
        ks[rows(c, tokens), :] = blocks[c][0:tokens, 0:width]
        vs[rows(c, tokens), :] = blocks[c][0:tokens, width : 2 * width]
    sums[...] = jnp.zeros_like(sums)

    def step(hs, size):
        seen = slice(0, size * tokens)
        for k, h in enumerate(hs):
            g = gn_ref[at(h, tokens), :]
            lanes = at(h, tokens)
            sums[seen, width : 2 * width] += nn(e_ref[seen, lanes], g)
            for c in range(size):
                r = rows(c, tokens)
                d = nt(vs[r, :], g) - dots_ref[0:1, lanes]
                ds[k][r, :] = (e_ref[r, lanes].astype(jnp.float32) * d).astype(jnp.bfloat16)
        for k, h in enumerate(hs):
            lanes = at(h, width)
            sums[seen, 0:width] += nn(ds[k][seen, :], q_ref[:, lanes])
            dq = far_dq[:, lanes] + tn(ds[k][seen, :], ks[seen, :])
            dq_ref[:, lanes] = (dq * scale).astype(dq_ref.dtype)

    for_heads(heads, jnp.sum(reach).astype(jnp.int32), NEAR_SIZES, step)
    sums[:, 0:width] = sums[:, 0:width] * scale


def add_parts(sums, far, *outs):
    tokens = outs[0].shape[0]
    for d, out in enumerate(outs):
        total = sums[rows(d + 1, tokens), :] + far[rows(d, tokens), :].astype(jnp.float32)
        out[...] = total.astype(out.dtype)


VM = pl.BlockSpec(memory_space=pltpu.VMEM)


def call(kernel, name, args, outs, scratch, flops):
    return pl.pallas_call(
        kernel,
        out_shape=tuple(jax.ShapeDtypeStruct(*o) for o in outs),
        in_specs=[VM] * len(args),
        out_specs=(VM,) * len(outs),
        scratch_shapes=[pltpu.VMEM(*s) for s in scratch],
        compiler_params=pltpu.CompilerParams(vmem_limit_bytes=24 * 1024 * 1024),
        cost_estimate=pl.CostEstimate(flops=flops, bytes_accessed=1 << 21, transcendentals=0),
        name=name,
    )(*args)


BF, F32 = jnp.bfloat16, jnp.float32


def dims(queries, own):
    tokens = queries.shape[0]
    width = own.shape[1] // 2
    return tokens, width, queries.shape[1] // width


def run_near_forward(queries, near):
    tokens, width, heads = dims(queries, near[0])
    keys, all_rows = (NEAR + 1) * tokens, heads * tokens
    return call(
        functools.partial(near_forward, heads),
        "near_forward",
        (queries, *near),
        [((keys, all_rows), BF), (queries.shape, F32), ((16, all_rows), F32)],
        [((keys, width), BF)] * 2 + [((keys, tokens), F32)] * (1 + GROUP),
        4 * keys * all_rows * width,
    )


def run_far(queries, out_grad, near_out, stats, own, far):
    tokens, width, heads = dims(queries, own)
    keys, all_rows = FAR * tokens, heads * tokens
    return call(
        functools.partial(far_both, heads),
        "far_both",
        (queries, out_grad, near_out, stats, own, far),
        [
            (queries.shape, BF),
            ((keys, 2 * width), BF),
            (queries.shape, F32),
            ((all_rows, width), BF),
            ((8, all_rows), F32),
        ],
        [((keys, width), BF)] * 2
        + [((keys, tokens), F32), ((keys, 2 * width), F32)]
        + [((keys, tokens), F32)] * GROUP
        + [((keys, tokens), BF)] * (2 * GROUP)
        + [((tokens, width), BF)] * GROUP
        + [((8, tokens), F32)] * GROUP,
        10 * keys * all_rows * width,
    )


def run_near_backward(queries, near_grad, dots, weights, far_dq, near):
    tokens, width, heads = dims(queries, near[0])
    keys, all_rows = (NEAR + 1) * tokens, heads * tokens
    return call(
        functools.partial(near_backward, heads),
        "near_backward",
        (queries, near_grad, dots, weights, far_dq, *near),
        [(queries.shape, BF), ((keys, 2 * width), F32)],
        [((keys, width), BF)] * 2 + [((keys, tokens), BF)] * GROUP,
        8 * keys * all_rows * width,
    )


def run_add(sums, far):
    tokens = far.shape[0] // FAR
    return call(add_parts, "add_parts", (sums, far), [((tokens, far.shape[1]), BF)] * NEAR, [], 1)


def on_device(queries, key_rows, value_rows, out_grad, segment):
    tokens, width = key_rows.shape
    marks = jnp.broadcast_to(segment.astype(jnp.bfloat16)[None, :], (16, tokens))
    own = jnp.concatenate([jnp.concatenate([key_rows, value_rows], axis=1), marks], axis=0)
    near = [own] + [wrapped(own, d) for d in range(1, NEAR + 1)]
    far = wrapped(jnp.concatenate(near[1:], axis=0), NEAR)
    weights, near_out, stats = run_near_forward(queries, near)
    attended, far_part, far_dq, near_grad, dots = run_far(
        queries, out_grad, near_out, stats, own, far
    )
    far_back = wrapped(far_part, -NEAR)
    query_grad, sums = run_near_backward(queries, near_grad, dots, weights, far_dq, near)
    total = sums[:tokens]
    for d, part in enumerate(run_add(sums, far_back)):
        total = total + wrapped(part, -d - 1).astype(jnp.float32)
    return attended, query_grad, total[:, :width], total[:, width:]


def solution(mesh):
    spec = P(AXES, None)
    return jax.shard_map(
        on_device,
        mesh=mesh,
        in_specs=(spec, spec, spec, spec, P(AXES)),
        out_specs=(spec,) * 4,
        check_vma=False,
    )
```

```python
import functools
import math

import jax
import jax.numpy as jnp
from jax import lax
from jax.experimental import pallas as pl
from jax.experimental.pallas import tpu as pltpu
from jax.sharding import PartitionSpec as P

AXES = ("seq", "grp")
NEAR = 3
FAR = 3
NEAR_SIZES = (2, 4)
FAR_SIZES = (0, 1, 3)
GROUP = 4
HIDE = -1e30


def wrapped(value, steps, axes=AXES):
    count = lax.axis_size(axes)
    return lax.ppermute(value, axes, [(i, (i + steps) % count) for i in range(count)])


def dot(a, b, over_a, over_b):
    return lax.dot_general(
        a, b, (((over_a,), (over_b,)), ((), ())), preferred_element_type=jnp.float32
    )


def nt(a, b):
    return dot(a, b, 1, 1)


def nn(a, b):
    return dot(a, b, 1, 0)


def tn(a, b):
    return dot(a, b, 0, 0)


def rows(c, size):
    return slice(c * size, (c + 1) * size)


def at(h, size):
    return pl.ds(pl.multiple_of(h * size, size), size)


def marks_of(block, tokens):
    return block[tokens : tokens + 8, :].astype(jnp.float32)


def reached(seg_row, first):
    return jnp.sum(jnp.where(seg_row == first, 1.0, 0.0), axis=1, keepdims=True)


def bias_of(seg_row, row_seg, first, key_at):
    tokens = key_at.shape[0]
    count = reached(seg_row, first)
    shown = (key_at.astype(jnp.float32) >= tokens - count) & (row_seg == first)
    return jnp.where(shown, 0.0, HIDE), jnp.where(count > 0, 1.0, 0.0)


def for_heads(heads, needed, sizes, step, finish=None):
    below = -1
    for size in sizes:

        @pl.when((needed > below) & (needed <= size))
        def _(size=size):
            def group(i, carry):
                step([i * GROUP + k for k in range(GROUP)], size)
                return carry

            lax.fori_loop(0, heads // GROUP, group, 0)
            if finish is not None:
                finish(size)

        below = size


def fold(op, x):
    return op(x.reshape(-1, 8, x.shape[1]), axis=0)


def own_scores(heads, q_ref, own, s_ref, top_ref, bias):
    tokens = q_ref.shape[0]
    width = q_ref.shape[1] // heads
    scale2 = width**-0.5 * math.log2(math.e)
    own_seg = marks_of(own, tokens)
    key_seg = jnp.transpose(own_seg)[:, 0:1]
    key_at = lax.broadcasted_iota(jnp.int32, (tokens, tokens), 0)
    row_at = lax.broadcasted_iota(jnp.int32, (tokens, tokens), 1)
    shown = (key_seg == own_seg[0:1, :]) & (key_at <= row_at)
    bias[...] = jnp.where(shown, 0.0, HIDE)

    def group(i, carry):
        for k in range(GROUP):
            h = i * GROUP + k
            q = q_ref[:, at(h, width)]
            s = nt(own[0:tokens, 0:width], q) * scale2 + bias[...]
            s_ref[:, at(h, tokens)] = s
            top_ref[:, at(h, tokens)] = fold(jnp.max, s)
        return carry

    lax.fori_loop(0, heads // GROUP, group, 0)


def near_forward(heads, q_ref, s_ref, top_ref, *refs):
    blocks = refs[: NEAR + 1]
    e_ref, o_ref, stat_ref, ks, vs, bias, *sc = refs[NEAR + 1 :]
    tokens = q_ref.shape[0]
    width = q_ref.shape[1] // heads
    scale2 = width**-0.5 * math.log2(math.e)
    row_seg = marks_of(blocks[0], tokens)[0:1, :]
    key_at = lax.broadcasted_iota(jnp.int32, (tokens, tokens), 0)
    first = row_seg[:, 0:1]
    reach = jnp.ones((1, 1), jnp.float32)
    for c in range(1, NEAR + 1):
        bias[rows(c - 1, tokens), :], more = bias_of(
            marks_of(blocks[c], tokens)[0:1, :], row_seg, first, key_at
        )
        reach = reach + more
    for c in range(NEAR + 1):
        ks[rows(c, tokens), :] = blocks[c][0:tokens, 0:width]
        vs[rows(c, tokens), :] = blocks[c][0:tokens, width : 2 * width]

    def step(hs, size):
        for k, h in enumerate(hs):
            q = q_ref[:, at(h, width)]
            top = top_ref[:, at(h, tokens)]
            for c in range(1, size):
                r = rows(c - 1, tokens)
                s = nt(ks[rows(c, tokens), :], q) * scale2 + bias[r, :]
                sc[k][r, :] = s
                top = jnp.maximum(top, fold(jnp.max, s))
            top = jnp.max(top, axis=0, keepdims=True)
            total = jnp.zeros((8, tokens), jnp.float32)
            for c in range(size):
                s = sc[k][rows(c - 1, tokens), :] if c else s_ref[:, at(h, tokens)]
                e = jnp.exp2(s - top)
                total = total + fold(jnp.sum, e)
                e_ref[rows(c, tokens), at(h, tokens)] = e.astype(jnp.bfloat16)
            total = jnp.sum(total, axis=0, keepdims=True)
            stat_ref[0:8, at(h, tokens)] = jnp.broadcast_to(top, (8, tokens))
            stat_ref[8:16, at(h, tokens)] = jnp.broadcast_to(total, (8, tokens))
        seen = slice(0, size * tokens)
        for h in hs:
            o_ref[:, at(h, width)] = tn(e_ref[seen, at(h, tokens)], vs[seen, :])

    for_heads(heads, jnp.sum(reach).astype(jnp.int32), NEAR_SIZES, step)


def far_both(heads, q_ref, g_ref, near_out, stat_ref, own, far, *refs):
    o_ref, part, dq_ref, gn_ref, dots_ref, ks, vs, bias, sums, *slots = refs
    sc, ex, ds, gf, dt = (slots[i * GROUP : (i + 1) * GROUP] for i in range(5))
    tokens = q_ref.shape[0]
    width = q_ref.shape[1] // heads
    scale = width**-0.5
    scale2 = scale * math.log2(math.e)
    pitch = far.shape[0] // FAR
    row_seg = marks_of(own, tokens)[0:1, :]
    first = row_seg[:, 0:1]
    key_at = lax.broadcasted_iota(jnp.int32, (tokens, tokens), 0)
    reach = jnp.zeros((1, 1), jnp.float32)
    for c in range(FAR):
        seg = far[c * pitch + tokens : c * pitch + tokens + 8, :].astype(jnp.float32)[0:1, :]
        bias[rows(c, tokens), :], more = bias_of(seg, row_seg, first, key_at)
        reach = reach + more
        ks[rows(c, tokens), :] = far[c * pitch : c * pitch + tokens, 0:width]
        vs[rows(c, tokens), :] = far[c * pitch : c * pitch + tokens, width : 2 * width]
    sums[...] = jnp.zeros_like(sums)

    def step(hs, size):
        seen = slice(0, size * tokens)
        for k, h in enumerate(hs):
            q = q_ref[:, at(h, width)]
            lanes = at(h, tokens)
            old = stat_ref[0:1, lanes]
            top = jnp.broadcast_to(old, (8, tokens))
            for c in range(size):
                r = rows(c, tokens)
                s = nt(ks[r, :], q) * scale2 + bias[r, :]
                sc[k][r, :] = s
                top = jnp.maximum(top, fold(jnp.max, s))
            top = jnp.max(top, axis=0, keepdims=True)
            keep = jnp.exp2(old - top)
            total = jnp.zeros((8, tokens), jnp.float32)
            for c in range(size):
                r = rows(c, tokens)
                e = jnp.exp2(sc[k][r, :] - top)
                total = total + fold(jnp.sum, e)
                ex[k][r, :] = e.astype(jnp.bfloat16)
            total = jnp.sum(total, axis=0, keepdims=True) + stat_ref[8:9, lanes] * keep
            inv = 1.0 / total
            near = inv * keep
            both = jnp.concatenate(
                [jnp.broadcast_to(inv, (8, tokens)), jnp.broadcast_to(near, (8, tokens))], axis=0
            )
            cols = jnp.transpose(both)
            inv_rows, near_rows = cols[:, 0:1], cols[:, 8:9]
            g = g_ref[:, at(h, width)].astype(jnp.float32)
            gf[k][...] = (g * inv_rows).astype(jnp.bfloat16)
            gn_ref[lanes, :] = (g * near_rows).astype(jnp.bfloat16)
            out = near_out[:, at(h, width)] * near_rows
            if size:
                out = out + tn(ex[k][seen, :], vs[seen, :]) * inv_rows
            o_ref[:, at(h, width)] = out.astype(o_ref.dtype)
            prod = g * out
            high = prod.astype(jnp.bfloat16)
            low = (prod - high.astype(jnp.float32)).astype(jnp.bfloat16)
            ones = jnp.ones((8, width), jnp.bfloat16)
            dots = nt(ones, high) + nt(ones, low)
            dots_ref[:, lanes] = dots * near
            dt[k][...] = dots * inv
        for k, h in enumerate(hs):
            lanes = at(h, width)
            if not size:
                dq_ref[:, lanes] = jnp.zeros((tokens, width), jnp.float32)
                continue
            q = q_ref[:, lanes]
            g = gf[k][...]
            sums[seen, width : 2 * width] += nn(ex[k][seen, :], g)
            for c in range(size):
                r = rows(c, tokens)
                d = nt(vs[r, :], g) - dt[k][0:1, :]
                ds[k][r, :] = (ex[k][r, :].astype(jnp.float32) * d).astype(jnp.bfloat16)
            sums[seen, 0:width] += nn(ds[k][seen, :], q)
            dq_ref[:, lanes] = tn(ds[k][seen, :], ks[seen, :])

    for_heads(heads, jnp.sum(reach).astype(jnp.int32), FAR_SIZES, step)
    part[:, 0:width] = (sums[:, 0:width] * scale).astype(part.dtype)
    part[:, width : 2 * width] = sums[:, width : 2 * width].astype(part.dtype)


def near_backward(heads, q_ref, gn_ref, dots_ref, e_ref, far_dq, *refs):
    blocks = refs[: NEAR + 1]
    dq_ref, sums, ks, vs, *ds = refs[NEAR + 1 :]
    tokens = q_ref.shape[0]
    width = q_ref.shape[1] // heads
    scale = width**-0.5
    row_seg = marks_of(blocks[0], tokens)[0:1, :]
    reach = jnp.ones((1, 1), jnp.float32)
    for c in range(1, NEAR + 1):
        count = reached(marks_of(blocks[c], tokens)[0:1, :], row_seg[:, 0:1])
        reach = reach + jnp.where(count > 0, 1.0, 0.0)
    for c in range(NEAR + 1):
        ks[rows(c, tokens), :] = blocks[c][0:tokens, 0:width]
        vs[rows(c, tokens), :] = blocks[c][0:tokens, width : 2 * width]
    sums[...] = jnp.zeros_like(sums)

    def step(hs, size):
        seen = slice(0, size * tokens)
        for k, h in enumerate(hs):
            g = gn_ref[at(h, tokens), :]
            lanes = at(h, tokens)
            for c in range(size):
                r = rows(c, tokens)
                d = nt(vs[r, :], g) - dots_ref[0:1, lanes]
                ds[k][r, :] = (e_ref[r, lanes].astype(jnp.float32) * d).astype(jnp.bfloat16)
        for k, h in enumerate(hs):
            lanes = at(h, width)
            sums[seen, 0:width] += nn(ds[k][seen, :], q_ref[:, lanes])
            dq = far_dq[:, lanes] + tn(ds[k][seen, :], ks[seen, :])
            dq_ref[:, lanes] = (dq * scale).astype(dq_ref.dtype)

    def finish(size):
        seen = slice(0, size * tokens)
        sums[seen, width : 2 * width] = nn(e_ref[seen, :], gn_ref[...])
        sums[seen, 0:width] = sums[seen, 0:width] * scale

    for_heads(heads, jnp.sum(reach).astype(jnp.int32), NEAR_SIZES, step, finish)


def add_parts(sums, far, own, *outs):
    tokens = own.shape[0]
    for d in range(FAR):
        out = outs[d - 1] if d else own
        total = sums[rows(d, tokens), :] + far[rows(d, tokens), :].astype(jnp.float32)
        out[...] = total.astype(out.dtype)


VM = pl.BlockSpec(memory_space=pltpu.VMEM)


def call(kernel, name, args, outs, scratch, flops):
    return pl.pallas_call(
        kernel,
        out_shape=tuple(jax.ShapeDtypeStruct(*o) for o in outs),
        in_specs=[VM] * len(args),
        out_specs=(VM,) * len(outs),
        scratch_shapes=[pltpu.VMEM(*s) for s in scratch],
        compiler_params=pltpu.CompilerParams(vmem_limit_bytes=24 * 1024 * 1024),
        cost_estimate=pl.CostEstimate(flops=flops, bytes_accessed=1 << 21, transcendentals=0),
        name=name,
    )(*args)


BF, F32 = jnp.bfloat16, jnp.float32


def dims(queries, own):
    tokens = queries.shape[0]
    width = own.shape[1] // 2
    return tokens, width, queries.shape[1] // width


def run_own(queries, own):
    tokens, width, heads = dims(queries, own)
    return call(
        functools.partial(own_scores, heads),
        "own_scores",
        (queries, own),
        [((tokens, heads * tokens), F32), ((8, heads * tokens), F32)],
        [((tokens, tokens), F32)],
        4 * tokens * heads * tokens * width,
    )


def run_near_forward(queries, scores, tops, near):
    tokens, width, heads = dims(queries, near[0])
    keys, all_rows = (NEAR + 1) * tokens, heads * tokens
    return call(
        functools.partial(near_forward, heads),
        "near_forward",
        (queries, scores, tops, *near),
        [((keys, all_rows), BF), (queries.shape, F32), ((16, all_rows), F32)],
        [((keys, width), BF)] * 2 + [((NEAR * tokens, tokens), F32)] * (1 + GROUP),
        4 * keys * all_rows * width,
    )


def run_far(queries, out_grad, near_out, stats, own, far):
    tokens, width, heads = dims(queries, own)
    keys, all_rows = FAR * tokens, heads * tokens
    return call(
        functools.partial(far_both, heads),
        "far_both",
        (queries, out_grad, near_out, stats, own, far),
        [
            (queries.shape, BF),
            ((keys, 2 * width), BF),
            (queries.shape, F32),
            ((all_rows, width), BF),
            ((8, all_rows), F32),
        ],
        [((keys, width), BF)] * 2
        + [((keys, tokens), F32), ((keys, 2 * width), F32)]
        + [((keys, tokens), F32)] * GROUP
        + [((keys, tokens), BF)] * (2 * GROUP)
        + [((tokens, width), BF)] * GROUP
        + [((8, tokens), F32)] * GROUP,
        10 * keys * all_rows * width,
    )


def run_near_backward(queries, near_grad, dots, weights, far_dq, near):
    tokens, width, heads = dims(queries, near[0])
    keys, all_rows = (NEAR + 1) * tokens, heads * tokens
    return call(
        functools.partial(near_backward, heads),
        "near_backward",
        (queries, near_grad, dots, weights, far_dq, *near),
        [(queries.shape, BF), ((keys, 2 * width), F32)],
        [((keys, width), BF)] * 2 + [((keys, tokens), BF)] * GROUP,
        8 * keys * all_rows * width,
    )


def run_add(sums, far):
    tokens = far.shape[0] // FAR
    one = (tokens, far.shape[1])
    return call(add_parts, "add_parts", (sums, far), [(one, F32)] + [(one, BF)] * (FAR - 1), [], 1)


def on_device(queries, key_rows, value_rows, out_grad, segment):
    tokens, width = key_rows.shape
    marks = jnp.broadcast_to(segment.astype(jnp.bfloat16)[None, :], (16, tokens))
    own = jnp.concatenate([jnp.concatenate([key_rows, value_rows], axis=1), marks], axis=0)
    near = [own] + [wrapped(own, d) for d in range(1, NEAR + 1)]
    far = wrapped(jnp.concatenate(near[:FAR], axis=0), 1, "seq")
    weights, near_out, stats = run_near_forward(queries, *run_own(queries, near[0]), near)
    attended, far_part, far_dq, near_grad, dots = run_far(
        queries, out_grad, near_out, stats, own, far
    )
    far_back = wrapped(far_part, -1, "seq")
    query_grad, sums = run_near_backward(queries, near_grad, dots, weights, far_dq, near)
    last = wrapped(sums[NEAR * tokens :].astype(jnp.bfloat16), -NEAR)
    total, *parts = run_add(sums, far_back)
    for d, part in enumerate(parts):
        total = total + wrapped(part, -d - 1).astype(jnp.float32)
    total = total + last.astype(jnp.float32)
    return attended, query_grad, total[:, :width], total[:, width:]


def solution(mesh):
    spec = P(AXES, None)
    return jax.shard_map(
        on_device,
        mesh=mesh,
        in_specs=(spec, spec, spec, spec, P(AXES)),
        out_specs=(spec,) * 4,
        check_vma=False,
    )
```

```python
import functools
import math

import jax
import jax.numpy as jnp
from jax import lax
from jax.experimental import pallas as pl
from jax.experimental.pallas import tpu as pltpu
from jax.sharding import PartitionSpec as P

AXES = ("seq", "grp")
NEAR = 2
FAR = 4
NEAR_SIZES = (2, 3)
FAR_SIZES = (0, 2, 4)
GROUP = 8
FAR_MIB = 28
HIDE = -1e30
BF, F32 = jnp.bfloat16, jnp.float32


def wrapped(value, steps, axes=AXES):
    count = lax.axis_size(axes)
    return lax.ppermute(value, axes, [(i, (i + steps) % count) for i in range(count)])


def dot(a, b, over_a, over_b):
    return lax.dot_general(
        a, b, (((over_a,), (over_b,)), ((), ())), preferred_element_type=jnp.float32
    )


def nt(a, b):
    return dot(a, b, 1, 1)


def nn(a, b):
    return dot(a, b, 1, 0)


def tn(a, b):
    return dot(a, b, 0, 0)


def rows(c, size):
    return slice(c * size, (c + 1) * size)


def at(h, size):
    return pl.ds(pl.multiple_of(h * size, size), size)


def marks_of(block, tokens):
    return block[tokens : tokens + 8, :].astype(jnp.float32)


def reached(seg_row, first):
    return jnp.sum(jnp.where(seg_row == first, 1.0, 0.0), axis=1, keepdims=True)


def bias_of(seg_row, row_seg, first, key_at):
    tokens = key_at.shape[0]
    count = reached(seg_row, first)
    shown = (key_at.astype(jnp.float32) >= tokens - count) & (row_seg == first)
    return jnp.where(shown, 0.0, HIDE), jnp.where(count > 0, 1.0, 0.0)


def for_heads(heads, needed, sizes, step, finish=None):
    below = -1
    for size in sizes:

        @pl.when((needed > below) & (needed <= size))
        def _(size=size):
            def group(i, carry):
                step([i * GROUP + k for k in range(GROUP)], size)
                return carry

            lax.fori_loop(0, heads // GROUP, group, 0)
            if finish is not None:
                finish(size)

        below = size


def fold(op, x):
    return op(x.reshape(-1, 8, x.shape[1]), axis=0)


def own_scores(heads, q_ref, own, s_ref, top_ref, qs_ref, bias):
    tokens = q_ref.shape[0]
    width = q_ref.shape[1] // heads
    scale2 = width**-0.5 * math.log2(math.e)
    own_seg = marks_of(own, tokens)
    key_seg = jnp.transpose(own_seg)[:, 0:1]
    key_at = lax.broadcasted_iota(jnp.int32, (tokens, tokens), 0)
    row_at = lax.broadcasted_iota(jnp.int32, (tokens, tokens), 1)
    shown = (key_seg == own_seg[0:1, :]) & (key_at <= row_at)
    bias[...] = jnp.where(shown, 0.0, HIDE)

    def group(i, carry):
        for k in range(GROUP):
            h = i * GROUP + k
            q = q_ref[:, at(h, width)]
            qs_ref[at(h, tokens), :] = q
            s = nt(own[0:tokens, 0:width], q) * scale2 + bias[...]
            s_ref[:, at(h, tokens)] = s
            top_ref[:, at(h, tokens)] = fold(jnp.max, s)
        return carry

    lax.fori_loop(0, heads // GROUP, group, 0)


def near_forward(heads, q_ref, s_ref, top_ref, *refs):
    blocks = refs[: NEAR + 1]
    e_ref, o_ref, stat_ref, ks, vs, bias, *sc = refs[NEAR + 1 :]
    tokens = q_ref.shape[0] // heads
    width = q_ref.shape[1]
    scale2 = width**-0.5 * math.log2(math.e)
    row_seg = marks_of(blocks[0], tokens)[0:1, :]
    key_at = lax.broadcasted_iota(jnp.int32, (tokens, tokens), 0)
    first = row_seg[:, 0:1]
    reach = jnp.ones((1, 1), jnp.float32)
    for c in range(1, NEAR + 1):
        bias[rows(c - 1, tokens), :], more = bias_of(
            marks_of(blocks[c], tokens)[0:1, :], row_seg, first, key_at
        )
        reach = reach + more
    for c in range(NEAR + 1):
        ks[rows(c, tokens), :] = blocks[c][0:tokens, 0:width]
        vs[rows(c, tokens), :] = blocks[c][0:tokens, width : 2 * width]

    def step(hs, size):
        for k, h in enumerate(hs):
            q = q_ref[at(h, tokens), :]
            top = top_ref[:, at(h, tokens)]
            for c in range(1, size):
                r = rows(c - 1, tokens)
                s = nt(ks[rows(c, tokens), :], q) * scale2 + bias[r, :]
                sc[k][r, :] = s
                top = jnp.maximum(top, fold(jnp.max, s))
            top = jnp.max(top, axis=0, keepdims=True)
            total = jnp.zeros((8, tokens), jnp.float32)
            for c in range(size):
                s = sc[k][rows(c - 1, tokens), :] if c else s_ref[:, at(h, tokens)]
                e = jnp.exp2(s - top)
                total = total + fold(jnp.sum, e)
                e_ref[rows(c, tokens), at(h, tokens)] = e.astype(jnp.bfloat16)
            total = jnp.sum(total, axis=0, keepdims=True)
            stat_ref[0:8, at(h, tokens)] = jnp.broadcast_to(top, (8, tokens))
            stat_ref[8:16, at(h, tokens)] = jnp.broadcast_to(total, (8, tokens))
        seen = slice(0, size * tokens)
        for h in hs:
            o_ref[:, at(h, width)] = tn(e_ref[seen, at(h, tokens)], vs[seen, :])

    for_heads(heads, jnp.sum(reach).astype(jnp.int32), NEAR_SIZES, step)


def far_both(heads, q_ref, g_ref, near_out, stat_ref, own, third, far, *refs):
    o_ref, third_part, part, dq_ref, gn_ref, dots_ref, ks, vs, bias, gf, dt, ex, ds, *sc = refs
    tokens = q_ref.shape[0] // heads
    width = q_ref.shape[1]
    scale = width**-0.5
    scale2 = scale * math.log2(math.e)
    pitch = third.shape[0]
    row_seg = marks_of(own, tokens)[0:1, :]
    first = row_seg[:, 0:1]
    key_at = lax.broadcasted_iota(jnp.int32, (tokens, tokens), 0)
    reach = jnp.zeros((1, 1), jnp.float32)
    for c in range(FAR):
        block = far.at[rows(c - 1, pitch), :] if c else third
        seg = marks_of(block, tokens)[0:1, :]
        bias[rows(c, tokens), :], more = bias_of(seg, row_seg, first, key_at)
        reach = reach + more
        ks[rows(c, tokens), :] = block[0:tokens, 0:width]
        vs[rows(c, tokens), :] = block[0:tokens, width : 2 * width]

    def step(hs, size):
        seen = slice(0, size * tokens)
        tops = []
        for k, h in enumerate(hs):
            q = q_ref[at(h, tokens), :]
            top = jnp.broadcast_to(stat_ref[0:1, at(h, tokens)], (8, tokens))
            for c in range(size):
                r = rows(c, tokens)
                s = nt(ks[r, :], q) * scale2 + bias[r, :]
                sc[k][r, :] = s
                top = jnp.maximum(top, fold(jnp.max, s))
            tops.append(jnp.max(top, axis=0, keepdims=True))
        invs = []
        for k, h in enumerate(hs):
            lanes = at(h, tokens)
            top = tops[k]
            keep = jnp.exp2(stat_ref[0:1, lanes] - top)
            total = jnp.zeros((8, tokens), jnp.float32)
            for c in range(size):
                r = rows(c, tokens)
                e = jnp.exp2(sc[k][r, :] - top)
                total = total + fold(jnp.sum, e)
                ex[r, lanes] = e.astype(jnp.bfloat16)
            total = jnp.sum(total, axis=0, keepdims=True) + stat_ref[8:9, lanes] * keep
            inv = 1.0 / total
            invs.append((inv, inv * keep))
        for k, h in enumerate(hs):
            lanes = at(h, tokens)
            inv, near = invs[k]
            both = jnp.concatenate(
                [jnp.broadcast_to(inv, (8, tokens)), jnp.broadcast_to(near, (8, tokens))], axis=0
            )
            cols = jnp.transpose(both)
            inv_rows, near_rows = cols[:, 0:1], cols[:, 8:9]
            g = g_ref[:, at(h, width)].astype(jnp.float32)
            gf[lanes, :] = (g * inv_rows).astype(jnp.bfloat16)
            gn_ref[lanes, :] = (g * near_rows).astype(jnp.bfloat16)
            out = near_out[:, at(h, width)] * near_rows
            if size:
                out = out + tn(ex[seen, lanes], vs[seen, :]) * inv_rows
            o_ref[:, at(h, width)] = out.astype(o_ref.dtype)
            prod = g * out
            high = prod.astype(jnp.bfloat16)
            low = (prod - high.astype(jnp.float32)).astype(jnp.bfloat16)
            ones = jnp.ones((8, width), jnp.bfloat16)
            dots = nt(ones, high) + nt(ones, low)
            dots_ref[:, lanes] = dots * near
            dt[:, lanes] = dots * inv
        if not size:
            return
        for h in hs:
            lanes = at(h, tokens)
            for c in range(size):
                r = rows(c, tokens)
                d = nt(vs[r, :], gf[lanes, :]) - dt[0:1, lanes]
                ds[r, lanes] = (ex[r, lanes].astype(jnp.float32) * d).astype(jnp.bfloat16)
        for h in hs:
            dq_ref[:, at(h, width)] = tn(ds[seen, at(h, tokens)], ks[seen, :])

    def finish(size):
        seen = slice(0, size * tokens)
        if size:
            values = nn(ex[seen, :], gf[...]).astype(part.dtype)
            keys = (nn(ds[seen, :], q_ref[...]) * scale).astype(part.dtype)
            third_part[:, 0:width] = keys[0:tokens, :]
            third_part[:, width : 2 * width] = values[0:tokens, :]
            part[0 : (size - 1) * tokens, 0:width] = keys[tokens:, :]
            part[0 : (size - 1) * tokens, width : 2 * width] = values[tokens:, :]
        else:
            dq_ref[...] = jnp.zeros_like(dq_ref)
            third_part[...] = jnp.zeros_like(third_part)
        if size < FAR:
            done = max(size - 1, 0) * tokens
            part[done:, :] = jnp.zeros((part.shape[0] - done, 2 * width), BF)

    for_heads(heads, jnp.sum(reach).astype(jnp.int32), FAR_SIZES, step, finish)


def near_backward(heads, q_ref, gn_ref, dots_ref, e_ref, far_dq, *refs):
    blocks = refs[: NEAR + 1]
    dq_ref, sums, ks, vs, ds = refs[NEAR + 1 :]
    tokens = q_ref.shape[0] // heads
    width = q_ref.shape[1]
    scale = width**-0.5
    row_seg = marks_of(blocks[0], tokens)[0:1, :]
    reach = jnp.ones((1, 1), jnp.float32)
    for c in range(1, NEAR + 1):
        count = reached(marks_of(blocks[c], tokens)[0:1, :], row_seg[:, 0:1])
        reach = reach + jnp.where(count > 0, 1.0, 0.0)
    for c in range(NEAR + 1):
        ks[rows(c, tokens), :] = blocks[c][0:tokens, 0:width]
        vs[rows(c, tokens), :] = blocks[c][0:tokens, width : 2 * width]

    def step(hs, size):
        seen = slice(0, size * tokens)
        for h in hs:
            g = gn_ref[at(h, tokens), :]
            lanes = at(h, tokens)
            for c in range(size):
                r = rows(c, tokens)
                d = nt(vs[r, :], g) - dots_ref[0:1, lanes]
                ds[r, lanes] = (e_ref[r, lanes].astype(jnp.float32) * d).astype(jnp.bfloat16)
        for h in hs:
            lanes = at(h, width)
            dq = far_dq[:, lanes] + tn(ds[seen, at(h, tokens)], ks[seen, :])
            dq_ref[:, lanes] = (dq * scale).astype(dq_ref.dtype)

    def finish(size):
        seen = slice(0, size * tokens)
        sums[seen, width : 2 * width] = nn(e_ref[seen, :], gn_ref[...])
        sums[seen, 0:width] = nn(ds[seen, :], q_ref[...]) * scale
        if size <= NEAR:
            sums[size * tokens :, :] = jnp.zeros((sums.shape[0] - size * tokens, 2 * width), F32)

    for_heads(heads, jnp.sum(reach).astype(jnp.int32), NEAR_SIZES, step, finish)


VM = pl.BlockSpec(memory_space=pltpu.VMEM)


def call(kernel, name, args, outs, scratch, flops, mib):
    return pl.pallas_call(
        kernel,
        out_shape=tuple(jax.ShapeDtypeStruct(*o) for o in outs),
        in_specs=[VM] * len(args),
        out_specs=(VM,) * len(outs),
        scratch_shapes=[pltpu.VMEM(*s) for s in scratch],
        compiler_params=pltpu.CompilerParams(vmem_limit_bytes=mib << 20),
        cost_estimate=pl.CostEstimate(flops=flops, bytes_accessed=1 << 21, transcendentals=0),
        name=name,
    )(*args)


def dims(queries, own):
    tokens = queries.shape[0]
    width = own.shape[1] // 2
    return tokens, width, queries.shape[1] // width


def run_own(queries, own):
    tokens, width, heads = dims(queries, own)
    return call(
        functools.partial(own_scores, heads),
        "own_scores",
        (queries, own),
        [
            ((tokens, heads * tokens), F32),
            ((8, heads * tokens), F32),
            ((heads * tokens, width), BF),
        ],
        [((tokens, tokens), F32)],
        4 * tokens * heads * tokens * width,
        8,
    )


def run_near_forward(stacked, scores, tops, near):
    tokens = near[0].shape[1]
    all_rows, width = stacked.shape
    keys = (NEAR + 1) * tokens
    return call(
        functools.partial(near_forward, all_rows // tokens),
        "near_forward",
        (stacked, scores, tops, *near),
        [((keys, all_rows), BF), ((tokens, all_rows // tokens * width), F32), ((16, all_rows), F32)],
        [((keys, width), BF)] * 2 + [((NEAR * tokens, tokens), F32)] * (1 + GROUP),
        4 * keys * all_rows * width,
        16,
    )


def run_far(stacked, out_grad, near_out, stats, own, third, far):
    tokens = out_grad.shape[0]
    all_rows, width = stacked.shape
    keys = FAR * tokens
    return call(
        functools.partial(far_both, all_rows // tokens),
        "far_both",
        (stacked, out_grad, near_out, stats, own, third, far),
        [
            (out_grad.shape, BF),
            ((tokens, 2 * width), BF),
            ((keys - tokens, 2 * width), BF),
            (out_grad.shape, F32),
            ((all_rows, width), BF),
            ((8, all_rows), F32),
        ],
        [((keys, width), BF)] * 2
        + [((keys, tokens), F32), ((all_rows, width), BF), ((8, all_rows), F32)]
        + [((keys, all_rows), BF)] * 2
        + [((keys, tokens), F32)] * GROUP,
        10 * keys * all_rows * width,
        FAR_MIB,
    )


def run_near_backward(stacked, near_grad, dots, weights, far_dq, near):
    tokens = far_dq.shape[0]
    all_rows, width = stacked.shape
    keys = (NEAR + 1) * tokens
    return call(
        functools.partial(near_backward, all_rows // tokens),
        "near_backward",
        (stacked, near_grad, dots, weights, far_dq, *near),
        [(far_dq.shape, BF), ((keys, 2 * width), F32)],
        [((keys, width), BF)] * 2 + [((keys, all_rows), BF)],
        8 * keys * all_rows * width,
        16,
    )


def pack_block(k_hbm, v_hbm, seg_hbm, out, seg, *sems):
    tokens, width = k_hbm.shape
    copies = (
        pltpu.make_async_copy(seg_hbm, seg, sems[0]),
        pltpu.make_async_copy(k_hbm, out.at[0:tokens, 0:width], sems[1]),
        pltpu.make_async_copy(v_hbm, out.at[0:tokens, width : 2 * width], sems[2]),
    )
    for copy in copies:
        copy.start()
    copies[0].wait()
    marks = jnp.broadcast_to(seg[...].astype(jnp.float32), (16, tokens))
    out[tokens : tokens + 16, :] = marks.astype(out.dtype)
    copies[1].wait()
    copies[2].wait()


def run_pack(key_rows, value_rows, segment):
    tokens, width = key_rows.shape
    return pl.pallas_call(
        pack_block,
        out_shape=jax.ShapeDtypeStruct((tokens + 16, 2 * width), BF),
        in_specs=[pl.BlockSpec(memory_space=pl.ANY)] * 3,
        out_specs=VM,
        scratch_shapes=[pltpu.VMEM((1, tokens), jnp.int32)] + [pltpu.SemaphoreType.DMA] * 3,
        compiler_params=pltpu.CompilerParams(vmem_limit_bytes=4 << 20),
        name="pack_block",
    )(key_rows, value_rows, segment.reshape(1, tokens))


def add_parts(sums, far, own, *outs):
    tokens = own.shape[0]
    for d in range(NEAR + 1):
        out = outs[d - 1] if d else own
        total = sums[rows(d, tokens), :] + far[rows(d, tokens), :].astype(F32)
        out[...] = total.astype(out.dtype)


def run_add(sums, far):
    one = (sums.shape[0] // (NEAR + 1), far.shape[1])
    return call(add_parts, "add_parts", (sums, far), [(one, F32)] + [(one, BF)] * NEAR, [], 1, 4)


def on_device(queries, key_rows, value_rows, out_grad, segment):
    width = key_rows.shape[1]
    own = run_pack(key_rows, value_rows, segment)
    near = [own] + [wrapped(own, d) for d in range(1, NEAR + 1)]
    third = wrapped(own, NEAR + 1)
    far = wrapped(jnp.concatenate(near, axis=0), 1, "seq")
    scores, tops, stacked = run_own(queries, own)
    weights, near_out, stats = run_near_forward(stacked, scores, tops, near)
    attended, third_part, far_part, far_dq, near_grad, dots = run_far(
        stacked, out_grad, near_out, stats, own, third, far
    )
    far_back = wrapped(far_part, -1, "seq")
    third_back = wrapped(third_part, -NEAR - 1)
    query_grad, sums = run_near_backward(stacked, near_grad, dots, weights, far_dq, near)
    total, *parts = run_add(sums, far_back)
    for d, part in enumerate(parts):
        total = total + wrapped(part, -d - 1).astype(F32)
    total = total + third_back.astype(F32)
    return attended, query_grad, total[:, :width], total[:, width:]


def solution(mesh):
    spec = P(AXES, None)
    return jax.shard_map(
        on_device,
        mesh=mesh,
        in_specs=(spec, spec, spec, spec, P(AXES)),
        out_specs=(spec,) * 4,
        check_vma=False,
    )
```

```python
import functools
import math

import jax
import jax.numpy as jnp
from jax import lax
from jax.experimental import pallas as pl
from jax.experimental.pallas import tpu as pltpu
from jax.sharding import PartitionSpec as P

AXES = ("seq", "grp")
NEAR = 3
FAR = 3
NEAR_SIZES = (2, 4)
FAR_SIZES = (0, 1, 3)
GROUP = 8
FAR_MIB = 28
HIDE = -1e30
BF, F32 = jnp.bfloat16, jnp.float32


def wrapped(value, steps, axes=AXES):
    count = lax.axis_size(axes)
    return lax.ppermute(value, axes, [(i, (i + steps) % count) for i in range(count)])


def dot(a, b, over_a, over_b):
    return lax.dot_general(
        a, b, (((over_a,), (over_b,)), ((), ())), preferred_element_type=jnp.float32
    )


def nt(a, b):
    return dot(a, b, 1, 1)


def nn(a, b):
    return dot(a, b, 1, 0)


def tn(a, b):
    return dot(a, b, 0, 0)


def rows(c, size):
    return slice(c * size, (c + 1) * size)


def at(h, size):
    return pl.ds(pl.multiple_of(h * size, size), size)


def marks_of(block, tokens):
    return block[tokens : tokens + 8, :].astype(jnp.float32)


def reached(seg_row, first):
    return jnp.sum(jnp.where(seg_row == first, 1.0, 0.0), axis=1, keepdims=True)


def bias_of(seg_row, row_seg, first, key_at):
    tokens = key_at.shape[0]
    count = reached(seg_row, first)
    shown = (key_at.astype(jnp.float32) >= tokens - count) & (row_seg == first)
    return jnp.where(shown, 0.0, HIDE), jnp.where(count > 0, 1.0, 0.0)


def for_heads(heads, needed, sizes, step, finish=None):
    below = -1
    for size in sizes:

        @pl.when((needed > below) & (needed <= size))
        def _(size=size):
            def group(i, carry):
                step([i * GROUP + k for k in range(GROUP)], size)
                return carry

            lax.fori_loop(0, heads // GROUP, group, 0)
            if finish is not None:
                finish(size)

        below = size


def fold(op, x):
    return op(x.reshape(-1, 8, x.shape[1]), axis=0)


def own_scores(heads, q_ref, own, s_ref, top_ref, qs_ref, bias):
    tokens = q_ref.shape[0]
    width = q_ref.shape[1] // heads
    scale2 = width**-0.5 * math.log2(math.e)
    own_seg = marks_of(own, tokens)
    key_seg = jnp.transpose(own_seg)[:, 0:1]
    key_at = lax.broadcasted_iota(jnp.int32, (tokens, tokens), 0)
    row_at = lax.broadcasted_iota(jnp.int32, (tokens, tokens), 1)
    shown = (key_seg == own_seg[0:1, :]) & (key_at <= row_at)
    bias[...] = jnp.where(shown, 0.0, HIDE)

    def group(i, carry):
        for k in range(GROUP):
            h = i * GROUP + k
            q = q_ref[:, at(h, width)]
            qs_ref[at(h, tokens), :] = q
            s = nt(own[0:tokens, 0:width], q) * scale2 + bias[...]
            s_ref[:, at(h, tokens)] = s
            top_ref[:, at(h, tokens)] = fold(jnp.max, s)
        return carry

    lax.fori_loop(0, heads // GROUP, group, 0)


def near_forward(heads, q_ref, s_ref, top_ref, *refs):
    blocks = refs[: NEAR + 1]
    e_ref, o_ref, stat_ref, ks, vs, bias, *sc = refs[NEAR + 1 :]
    tokens = q_ref.shape[0] // heads
    width = q_ref.shape[1]
    scale2 = width**-0.5 * math.log2(math.e)
    row_seg = marks_of(blocks[0], tokens)[0:1, :]
    key_at = lax.broadcasted_iota(jnp.int32, (tokens, tokens), 0)
    first = row_seg[:, 0:1]
    reach = jnp.ones((1, 1), jnp.float32)
    for c in range(1, NEAR + 1):
        bias[rows(c - 1, tokens), :], more = bias_of(
            marks_of(blocks[c], tokens)[0:1, :], row_seg, first, key_at
        )
        reach = reach + more
    for c in range(NEAR + 1):
        ks[rows(c, tokens), :] = blocks[c][0:tokens, 0:width]
        vs[rows(c, tokens), :] = blocks[c][0:tokens, width : 2 * width]

    def step(hs, size):
        for k, h in enumerate(hs):
            q = q_ref[at(h, tokens), :]
            top = top_ref[:, at(h, tokens)]
            for c in range(1, size):
                r = rows(c - 1, tokens)
                s = nt(ks[rows(c, tokens), :], q) * scale2 + bias[r, :]
                sc[k][r, :] = s
                top = jnp.maximum(top, fold(jnp.max, s))
            top = jnp.max(top, axis=0, keepdims=True)
            total = jnp.zeros((8, tokens), jnp.float32)
            for c in range(size):
                s = sc[k][rows(c - 1, tokens), :] if c else s_ref[:, at(h, tokens)]
                e = jnp.exp2(s - top)
                total = total + fold(jnp.sum, e)
                e_ref[rows(c, tokens), at(h, tokens)] = e.astype(jnp.bfloat16)
            total = jnp.sum(total, axis=0, keepdims=True)
            stat_ref[0:8, at(h, tokens)] = jnp.broadcast_to(top, (8, tokens))
            stat_ref[8:16, at(h, tokens)] = jnp.broadcast_to(total, (8, tokens))
        seen = slice(0, size * tokens)
        for h in hs:
            o_ref[:, at(h, width)] = tn(e_ref[seen, at(h, tokens)], vs[seen, :])

    for_heads(heads, jnp.sum(reach).astype(jnp.int32), NEAR_SIZES, step)


def far_both(heads, q_ref, g_ref, near_out, stat_ref, own, far, *refs):
    o_ref, part, dq_ref, gn_ref, dots_ref, ks, vs, bias, gf, dt, ex, ds, *sc = refs
    tokens = q_ref.shape[0] // heads
    width = q_ref.shape[1]
    scale = width**-0.5
    scale2 = scale * math.log2(math.e)
    pitch = far.shape[0] // FAR
    row_seg = marks_of(own, tokens)[0:1, :]
    first = row_seg[:, 0:1]
    key_at = lax.broadcasted_iota(jnp.int32, (tokens, tokens), 0)
    reach = jnp.zeros((1, 1), jnp.float32)
    for c in range(FAR):
        seg = far[c * pitch + tokens : c * pitch + tokens + 8, :].astype(jnp.float32)[0:1, :]
        bias[rows(c, tokens), :], more = bias_of(seg, row_seg, first, key_at)
        reach = reach + more
        ks[rows(c, tokens), :] = far[c * pitch : c * pitch + tokens, 0:width]
        vs[rows(c, tokens), :] = far[c * pitch : c * pitch + tokens, width : 2 * width]

    def step(hs, size):
        seen = slice(0, size * tokens)
        tops = []
        for k, h in enumerate(hs):
            q = q_ref[at(h, tokens), :]
            top = jnp.broadcast_to(stat_ref[0:1, at(h, tokens)], (8, tokens))
            for c in range(size):
                r = rows(c, tokens)
                s = nt(ks[r, :], q) * scale2 + bias[r, :]
                sc[k][r, :] = s
                top = jnp.maximum(top, fold(jnp.max, s))
            tops.append(jnp.max(top, axis=0, keepdims=True))
        invs = []
        for k, h in enumerate(hs):
            lanes = at(h, tokens)
            top = tops[k]
            keep = jnp.exp2(stat_ref[0:1, lanes] - top)
            total = jnp.zeros((8, tokens), jnp.float32)
            for c in range(size):
                r = rows(c, tokens)
                e = jnp.exp2(sc[k][r, :] - top)
                total = total + fold(jnp.sum, e)
                ex[r, lanes] = e.astype(jnp.bfloat16)
            total = jnp.sum(total, axis=0, keepdims=True) + stat_ref[8:9, lanes] * keep
            inv = 1.0 / total
            invs.append((inv, inv * keep))
        for k, h in enumerate(hs):
            lanes = at(h, tokens)
            inv, near = invs[k]
            both = jnp.concatenate(
                [jnp.broadcast_to(inv, (8, tokens)), jnp.broadcast_to(near, (8, tokens))], axis=0
            )
            cols = jnp.transpose(both)
            inv_rows, near_rows = cols[:, 0:1], cols[:, 8:9]
            g = g_ref[:, at(h, width)].astype(jnp.float32)
            gf[lanes, :] = (g * inv_rows).astype(jnp.bfloat16)
            gn_ref[lanes, :] = (g * near_rows).astype(jnp.bfloat16)
            out = near_out[:, at(h, width)] * near_rows
            if size:
                out = out + tn(ex[seen, lanes], vs[seen, :]) * inv_rows
            o_ref[:, at(h, width)] = out.astype(o_ref.dtype)
            prod = g * out
            high = prod.astype(jnp.bfloat16)
            low = (prod - high.astype(jnp.float32)).astype(jnp.bfloat16)
            ones = jnp.ones((8, width), jnp.bfloat16)
            dots = nt(ones, high) + nt(ones, low)
            dots_ref[:, lanes] = dots * near
            dt[:, lanes] = dots * inv
        if not size:
            return
        for h in hs:
            lanes = at(h, tokens)
            for c in range(size):
                r = rows(c, tokens)
                d = nt(vs[r, :], gf[lanes, :]) - dt[0:1, lanes]
                ds[r, lanes] = (ex[r, lanes].astype(jnp.float32) * d).astype(jnp.bfloat16)
        for h in hs:
            dq_ref[:, at(h, width)] = tn(ds[seen, at(h, tokens)], ks[seen, :])

    def finish(size):
        seen = slice(0, size * tokens)
        if size:
            values = nn(ex[seen, :], gf[...])
            part[seen, width : 2 * width] = values.astype(part.dtype)
            part[seen, 0:width] = (nn(ds[seen, :], q_ref[...]) * scale).astype(part.dtype)
        else:
            dq_ref[...] = jnp.zeros_like(dq_ref)
        if size < FAR:
            part[size * tokens :, :] = jnp.zeros((part.shape[0] - size * tokens, 2 * width), BF)

    for_heads(heads, jnp.sum(reach).astype(jnp.int32), FAR_SIZES, step, finish)


def near_backward(heads, q_ref, gn_ref, dots_ref, e_ref, far_dq, *refs):
    blocks = refs[: NEAR + 1]
    dq_ref, sums, ks, vs, ds = refs[NEAR + 1 :]
    tokens = q_ref.shape[0] // heads
    width = q_ref.shape[1]
    scale = width**-0.5
    row_seg = marks_of(blocks[0], tokens)[0:1, :]
    reach = jnp.ones((1, 1), jnp.float32)
    for c in range(1, NEAR + 1):
        count = reached(marks_of(blocks[c], tokens)[0:1, :], row_seg[:, 0:1])
        reach = reach + jnp.where(count > 0, 1.0, 0.0)
    for c in range(NEAR + 1):
        ks[rows(c, tokens), :] = blocks[c][0:tokens, 0:width]
        vs[rows(c, tokens), :] = blocks[c][0:tokens, width : 2 * width]

    def step(hs, size):
        seen = slice(0, size * tokens)
        for h in hs:
            g = gn_ref[at(h, tokens), :]
            lanes = at(h, tokens)
            for c in range(size):
                r = rows(c, tokens)
                d = nt(vs[r, :], g) - dots_ref[0:1, lanes]
                ds[r, lanes] = (e_ref[r, lanes].astype(jnp.float32) * d).astype(jnp.bfloat16)
        for h in hs:
            lanes = at(h, width)
            dq = far_dq[:, lanes] + tn(ds[seen, at(h, tokens)], ks[seen, :])
            dq_ref[:, lanes] = (dq * scale).astype(dq_ref.dtype)

    def finish(size):
        seen = slice(0, size * tokens)
        sums[seen, width : 2 * width] = nn(e_ref[seen, :], gn_ref[...])
        sums[seen, 0:width] = nn(ds[seen, :], q_ref[...]) * scale
        if size <= NEAR:
            sums[size * tokens :, :] = jnp.zeros((sums.shape[0] - size * tokens, 2 * width), F32)

    for_heads(heads, jnp.sum(reach).astype(jnp.int32), NEAR_SIZES, step, finish)


VM = pl.BlockSpec(memory_space=pltpu.VMEM)


def call(kernel, name, args, outs, scratch, flops, mib):
    return pl.pallas_call(
        kernel,
        out_shape=tuple(jax.ShapeDtypeStruct(*o) for o in outs),
        in_specs=[VM] * len(args),
        out_specs=(VM,) * len(outs),
        scratch_shapes=[pltpu.VMEM(*s) for s in scratch],
        compiler_params=pltpu.CompilerParams(vmem_limit_bytes=mib << 20),
        cost_estimate=pl.CostEstimate(flops=flops, bytes_accessed=1 << 21, transcendentals=0),
        name=name,
    )(*args)


def dims(queries, own):
    tokens = queries.shape[0]
    width = own.shape[1] // 2
    return tokens, width, queries.shape[1] // width


def run_own(queries, own):
    tokens, width, heads = dims(queries, own)
    return call(
        functools.partial(own_scores, heads),
        "own_scores",
        (queries, own),
        [
            ((tokens, heads * tokens), F32),
            ((8, heads * tokens), F32),
            ((heads * tokens, width), BF),
        ],
        [((tokens, tokens), F32)],
        4 * tokens * heads * tokens * width,
        8,
    )


def run_near_forward(stacked, scores, tops, near):
    tokens = near[0].shape[1]
    all_rows, width = stacked.shape
    keys = (NEAR + 1) * tokens
    return call(
        functools.partial(near_forward, all_rows // tokens),
        "near_forward",
        (stacked, scores, tops, *near),
        [((keys, all_rows), BF), ((tokens, all_rows // tokens * width), F32), ((16, all_rows), F32)],
        [((keys, width), BF)] * 2 + [((NEAR * tokens, tokens), F32)] * (1 + GROUP),
        4 * keys * all_rows * width,
        16,
    )


def run_far(stacked, out_grad, near_out, stats, own, far):
    tokens = out_grad.shape[0]
    all_rows, width = stacked.shape
    keys = FAR * tokens
    return call(
        functools.partial(far_both, all_rows // tokens),
        "far_both",
        (stacked, out_grad, near_out, stats, own, far),
        [
            (out_grad.shape, BF),
            ((keys, 2 * width), BF),
            (out_grad.shape, F32),
            ((all_rows, width), BF),
            ((8, all_rows), F32),
        ],
        [((keys, width), BF)] * 2
        + [((keys, tokens), F32), ((all_rows, width), BF), ((8, all_rows), F32)]
        + [((keys, all_rows), BF)] * 2
        + [((keys, tokens), F32)] * GROUP,
        10 * keys * all_rows * width,
        FAR_MIB,
    )


def run_near_backward(stacked, near_grad, dots, weights, far_dq, near):
    tokens = far_dq.shape[0]
    all_rows, width = stacked.shape
    keys = (NEAR + 1) * tokens
    return call(
        functools.partial(near_backward, all_rows // tokens),
        "near_backward",
        (stacked, near_grad, dots, weights, far_dq, *near),
        [(far_dq.shape, BF), ((keys, 2 * width), F32)],
        [((keys, width), BF)] * 2 + [((keys, all_rows), BF)],
        8 * keys * all_rows * width,
        16,
    )


def pack_block(k_hbm, v_hbm, seg_hbm, out, seg, *sems):
    tokens, width = k_hbm.shape
    copies = (
        pltpu.make_async_copy(seg_hbm, seg, sems[0]),
        pltpu.make_async_copy(k_hbm, out.at[0:tokens, 0:width], sems[1]),
        pltpu.make_async_copy(v_hbm, out.at[0:tokens, width : 2 * width], sems[2]),
    )
    for copy in copies:
        copy.start()
    copies[0].wait()
    marks = jnp.broadcast_to(seg[...].astype(jnp.float32), (16, tokens))
    out[tokens : tokens + 16, :] = marks.astype(out.dtype)
    copies[1].wait()
    copies[2].wait()


def run_pack(key_rows, value_rows, segment):
    tokens, width = key_rows.shape
    return pl.pallas_call(
        pack_block,
        out_shape=jax.ShapeDtypeStruct((tokens + 16, 2 * width), BF),
        in_specs=[pl.BlockSpec(memory_space=pl.ANY)] * 3,
        out_specs=VM,
        scratch_shapes=[pltpu.VMEM((1, tokens), jnp.int32)] + [pltpu.SemaphoreType.DMA] * 3,
        compiler_params=pltpu.CompilerParams(vmem_limit_bytes=62 << 20),
        name="pack_block",
    )(key_rows, value_rows, segment.reshape(1, tokens))


def add_parts(sums, far, own, *outs):
    tokens = own.shape[0]
    for d in range(FAR):
        out = outs[d - 1] if d else own
        total = sums[rows(d, tokens), :] + far[rows(d, tokens), :].astype(F32)
        out[...] = total.astype(out.dtype)


def run_add(sums, far):
    one = (far.shape[0] // FAR, far.shape[1])
    outs = [(one, F32)] + [(one, BF)] * (FAR - 1)
    return call(add_parts, "add_parts", (sums, far), outs, [], 1, 4)


def on_device(queries, key_rows, value_rows, out_grad, segment):
    tokens, width = key_rows.shape
    own = run_pack(key_rows, value_rows, segment)
    near = [own] + [wrapped(own, d) for d in range(1, NEAR + 1)]
    near[1:] = lax.optimization_barrier(near[1:])
    far = wrapped(jnp.concatenate(near[:FAR], axis=0), 1, "seq")
    scores, tops, stacked = run_own(queries, own)
    weights, near_out, stats = run_near_forward(stacked, scores, tops, near)
    attended, far_part, far_dq, near_grad, dots = run_far(
        stacked, out_grad, near_out, stats, own, far
    )
    far_back = wrapped(far_part, -1, "seq")
    query_grad, sums = run_near_backward(stacked, near_grad, dots, weights, far_dq, near)
    last = wrapped(sums[NEAR * tokens :].astype(BF), -NEAR)
    total, *parts = run_add(sums, far_back)
    for d, part in enumerate(parts):
        total = total + wrapped(part, -d - 1).astype(F32)
    total = total + last.astype(F32)
    return attended, query_grad, total[:, :width], total[:, width:]


def solution(mesh):
    spec = P(AXES, None)
    return jax.shard_map(
        on_device,
        mesh=mesh,
        in_specs=(spec, spec, spec, spec, P(AXES)),
        out_specs=(spec,) * 4,
        check_vma=False,
    )
```

```python
import functools
import math

import jax
import jax.numpy as jnp
from jax import lax
from jax.experimental import pallas as pl
from jax.experimental.pallas import tpu as pltpu
from jax.sharding import PartitionSpec as P

AXES = ("seq", "grp")
NEAR = 3
FAR = 3
NEAR_SIZES = (2, 4)
FAR_SIZES = (0, 1, 3)
GROUP = 8
FAR_MIB = 28
HIDE = -1e30
BF, F32 = jnp.bfloat16, jnp.float32


def wrapped(value, steps, axes=AXES):
    count = lax.axis_size(axes)
    return lax.ppermute(value, axes, [(i, (i + steps) % count) for i in range(count)])


def dot(a, b, over_a, over_b):
    return lax.dot_general(
        a, b, (((over_a,), (over_b,)), ((), ())), preferred_element_type=jnp.float32
    )


def nt(a, b):
    return dot(a, b, 1, 1)


def nn(a, b):
    return dot(a, b, 1, 0)


def tn(a, b):
    return dot(a, b, 0, 0)


def rows(c, size):
    return slice(c * size, (c + 1) * size)


def at(h, size):
    return pl.ds(pl.multiple_of(h * size, size), size)


def marks_of(block, tokens):
    return block[tokens : tokens + 8, :].astype(jnp.float32)


def reached(seg_row, first):
    return jnp.sum(jnp.where(seg_row == first, 1.0, 0.0), axis=1, keepdims=True)


def bias_of(seg_row, row_seg, first, key_at):
    tokens = key_at.shape[0]
    count = reached(seg_row, first)
    shown = (key_at.astype(jnp.float32) >= tokens - count) & (row_seg == first)
    return jnp.where(shown, 0.0, HIDE), jnp.where(count > 0, 1.0, 0.0)


def for_heads(heads, needed, sizes, step, finish=None):
    below = -1
    for size in sizes:

        @pl.when((needed > below) & (needed <= size))
        def _(size=size):
            def group(i, carry):
                step([i * GROUP + k for k in range(GROUP)], size)
                return carry

            lax.fori_loop(0, heads // GROUP, group, 0)
            if finish is not None:
                finish(size)

        below = size


def fold(op, x):
    return op(x.reshape(-1, 8, x.shape[1]), axis=0)


def own_scores(heads, q_ref, own, s_ref, top_ref, qs_ref, held, bias):
    held[...] = own[...]
    tokens = q_ref.shape[0]
    width = q_ref.shape[1] // heads
    scale2 = width**-0.5 * math.log2(math.e)
    own_seg = marks_of(own, tokens)
    key_seg = jnp.transpose(own_seg)[:, 0:1]
    key_at = lax.broadcasted_iota(jnp.int32, (tokens, tokens), 0)
    row_at = lax.broadcasted_iota(jnp.int32, (tokens, tokens), 1)
    shown = (key_seg == own_seg[0:1, :]) & (key_at <= row_at)
    bias[...] = jnp.where(shown, 0.0, HIDE)

    def group(i, carry):
        for k in range(GROUP):
            h = i * GROUP + k
            q = q_ref[:, at(h, width)]
            qs_ref[at(h, tokens), :] = q
            s = nt(own[0:tokens, 0:width], q) * scale2 + bias[...]
            s_ref[:, at(h, tokens)] = s
            top_ref[:, at(h, tokens)] = fold(jnp.max, s)
        return carry

    lax.fori_loop(0, heads // GROUP, group, 0)


def near_forward(heads, q_ref, s_ref, top_ref, *refs):
    blocks = refs[: NEAR + 1]
    e_ref, o_ref, stat_ref, ks, vs, bias, *sc = refs[NEAR + 1 :]
    tokens = q_ref.shape[0] // heads
    width = q_ref.shape[1]
    scale2 = width**-0.5 * math.log2(math.e)
    row_seg = marks_of(blocks[0], tokens)[0:1, :]
    key_at = lax.broadcasted_iota(jnp.int32, (tokens, tokens), 0)
    first = row_seg[:, 0:1]
    reach = jnp.ones((1, 1), jnp.float32)
    for c in range(1, NEAR + 1):
        bias[rows(c - 1, tokens), :], more = bias_of(
            marks_of(blocks[c], tokens)[0:1, :], row_seg, first, key_at
        )
        reach = reach + more
    for c in range(NEAR + 1):
        ks[rows(c, tokens), :] = blocks[c][0:tokens, 0:width]
        vs[rows(c, tokens), :] = blocks[c][0:tokens, width : 2 * width]

    def step(hs, size):
        for k, h in enumerate(hs):
            q = q_ref[at(h, tokens), :]
            top = top_ref[:, at(h, tokens)]
            for c in range(1, size):
                r = rows(c - 1, tokens)
                s = nt(ks[rows(c, tokens), :], q) * scale2 + bias[r, :]
                sc[k][r, :] = s
                top = jnp.maximum(top, fold(jnp.max, s))
            top = jnp.max(top, axis=0, keepdims=True)
            total = jnp.zeros((8, tokens), jnp.float32)
            for c in range(size):
                s = sc[k][rows(c - 1, tokens), :] if c else s_ref[:, at(h, tokens)]
                e = jnp.exp2(s - top)
                total = total + fold(jnp.sum, e)
                e_ref[rows(c, tokens), at(h, tokens)] = e.astype(jnp.bfloat16)
            total = jnp.sum(total, axis=0, keepdims=True)
            stat_ref[0:8, at(h, tokens)] = jnp.broadcast_to(top, (8, tokens))
            stat_ref[8:16, at(h, tokens)] = jnp.broadcast_to(total, (8, tokens))
        seen = slice(0, size * tokens)
        for h in hs:
            o_ref[:, at(h, width)] = tn(e_ref[seen, at(h, tokens)], vs[seen, :])

    for_heads(heads, jnp.sum(reach).astype(jnp.int32), NEAR_SIZES, step)


def far_both(heads, q_ref, g_ref, near_out, stat_ref, own, far, *refs):
    o_ref, part, dq_ref, gn_ref, dots_ref, ks, vs, bias, gf, dt, ex, ds, *sc = refs
    tokens = q_ref.shape[0] // heads
    width = q_ref.shape[1]
    scale = width**-0.5
    scale2 = scale * math.log2(math.e)
    pitch = far.shape[0] // FAR
    row_seg = marks_of(own, tokens)[0:1, :]
    first = row_seg[:, 0:1]
    key_at = lax.broadcasted_iota(jnp.int32, (tokens, tokens), 0)
    reach = jnp.zeros((1, 1), jnp.float32)
    for c in range(FAR):
        seg = far[c * pitch + tokens : c * pitch + tokens + 8, :].astype(jnp.float32)[0:1, :]
        bias[rows(c, tokens), :], more = bias_of(seg, row_seg, first, key_at)
        reach = reach + more
        ks[rows(c, tokens), :] = far[c * pitch : c * pitch + tokens, 0:width]
        vs[rows(c, tokens), :] = far[c * pitch : c * pitch + tokens, width : 2 * width]

    def step(hs, size):
        seen = slice(0, size * tokens)
        tops = []
        for k, h in enumerate(hs):
            q = q_ref[at(h, tokens), :]
            top = jnp.broadcast_to(stat_ref[0:1, at(h, tokens)], (8, tokens))
            for c in range(size):
                r = rows(c, tokens)
                s = nt(ks[r, :], q) * scale2 + bias[r, :]
                sc[k][r, :] = s
                top = jnp.maximum(top, fold(jnp.max, s))
            tops.append(jnp.max(top, axis=0, keepdims=True))
        invs = []
        for k, h in enumerate(hs):
            lanes = at(h, tokens)
            top = tops[k]
            keep = jnp.exp2(stat_ref[0:1, lanes] - top)
            total = jnp.zeros((8, tokens), jnp.float32)
            for c in range(size):
                r = rows(c, tokens)
                e = jnp.exp2(sc[k][r, :] - top)
                total = total + fold(jnp.sum, e)
                ex[r, lanes] = e.astype(jnp.bfloat16)
            total = jnp.sum(total, axis=0, keepdims=True) + stat_ref[8:9, lanes] * keep
            inv = 1.0 / total
            invs.append((inv, inv * keep))
        for k, h in enumerate(hs):
            lanes = at(h, tokens)
            inv, near = invs[k]
            both = jnp.concatenate(
                [jnp.broadcast_to(inv, (8, tokens)), jnp.broadcast_to(near, (8, tokens))], axis=0
            )
            cols = jnp.transpose(both)
            inv_rows, near_rows = cols[:, 0:1], cols[:, 8:9]
            g = g_ref[:, at(h, width)].astype(jnp.float32)
            gf[lanes, :] = (g * inv_rows).astype(jnp.bfloat16)
            gn_ref[lanes, :] = (g * near_rows).astype(jnp.bfloat16)
            out = near_out[:, at(h, width)] * near_rows
            if size:
                out = out + tn(ex[seen, lanes], vs[seen, :]) * inv_rows
            o_ref[:, at(h, width)] = out.astype(o_ref.dtype)
            prod = g * out
            high = prod.astype(jnp.bfloat16)
            low = (prod - high.astype(jnp.float32)).astype(jnp.bfloat16)
            ones = jnp.ones((8, width), jnp.bfloat16)
            dots = nt(ones, high) + nt(ones, low)
            dots_ref[:, lanes] = dots * near
            dt[:, lanes] = dots * inv
        if not size:
            return
        for h in hs:
            lanes = at(h, tokens)
            for c in range(size):
                r = rows(c, tokens)
                d = nt(vs[r, :], gf[lanes, :]) - dt[0:1, lanes]
                ds[r, lanes] = (ex[r, lanes].astype(jnp.float32) * d).astype(jnp.bfloat16)
        for h in hs:
            dq_ref[:, at(h, width)] = tn(ds[seen, at(h, tokens)], ks[seen, :])

    def finish(size):
        seen = slice(0, size * tokens)
        if size:
            values = nn(ex[seen, :], gf[...])
            part[seen, width : 2 * width] = values.astype(part.dtype)
            part[seen, 0:width] = (nn(ds[seen, :], q_ref[...]) * scale).astype(part.dtype)
        else:
            dq_ref[...] = jnp.zeros_like(dq_ref)
        if size < FAR:
            part[size * tokens :, :] = jnp.zeros((part.shape[0] - size * tokens, 2 * width), BF)

    for_heads(heads, jnp.sum(reach).astype(jnp.int32), FAR_SIZES, step, finish)


def near_backward(heads, q_ref, gn_ref, dots_ref, e_ref, far_dq, *refs):
    blocks = refs[: NEAR + 1]
    dq_ref, sums, ks, vs, ds = refs[NEAR + 1 :]
    tokens = q_ref.shape[0] // heads
    width = q_ref.shape[1]
    scale = width**-0.5
    row_seg = marks_of(blocks[0], tokens)[0:1, :]
    reach = jnp.ones((1, 1), jnp.float32)
    for c in range(1, NEAR + 1):
        count = reached(marks_of(blocks[c], tokens)[0:1, :], row_seg[:, 0:1])
        reach = reach + jnp.where(count > 0, 1.0, 0.0)
    for c in range(NEAR + 1):
        ks[rows(c, tokens), :] = blocks[c][0:tokens, 0:width]
        vs[rows(c, tokens), :] = blocks[c][0:tokens, width : 2 * width]

    def step(hs, size):
        seen = slice(0, size * tokens)
        for h in hs:
            g = gn_ref[at(h, tokens), :]
            lanes = at(h, tokens)
            for c in range(size):
                r = rows(c, tokens)
                d = nt(vs[r, :], g) - dots_ref[0:1, lanes]
                ds[r, lanes] = (e_ref[r, lanes].astype(jnp.float32) * d).astype(jnp.bfloat16)
        for h in hs:
            lanes = at(h, width)
            dq = far_dq[:, lanes] + tn(ds[seen, at(h, tokens)], ks[seen, :])
            dq_ref[:, lanes] = (dq * scale).astype(dq_ref.dtype)

    def finish(size):
        seen = slice(0, size * tokens)
        sums[seen, width : 2 * width] = nn(e_ref[seen, :], gn_ref[...])
        sums[seen, 0:width] = nn(ds[seen, :], q_ref[...]) * scale
        if size <= NEAR:
            sums[size * tokens :, :] = jnp.zeros((sums.shape[0] - size * tokens, 2 * width), F32)

    for_heads(heads, jnp.sum(reach).astype(jnp.int32), NEAR_SIZES, step, finish)


VM = pl.BlockSpec(memory_space=pltpu.VMEM)


def call(kernel, name, args, outs, scratch, flops, mib):
    return pl.pallas_call(
        kernel,
        out_shape=tuple(jax.ShapeDtypeStruct(*o) for o in outs),
        in_specs=[VM] * len(args),
        out_specs=(VM,) * len(outs),
        scratch_shapes=[pltpu.VMEM(*s) for s in scratch],
        compiler_params=pltpu.CompilerParams(vmem_limit_bytes=mib << 20),
        cost_estimate=pl.CostEstimate(flops=flops, bytes_accessed=1 << 21, transcendentals=0),
        name=name,
    )(*args)


def dims(queries, own):
    tokens = queries.shape[0]
    width = own.shape[1] // 2
    return tokens, width, queries.shape[1] // width


def run_own(queries, own):
    tokens, width, heads = dims(queries, own)
    return call(
        functools.partial(own_scores, heads),
        "own_scores",
        (queries, own),
        [
            ((tokens, heads * tokens), F32),
            ((8, heads * tokens), F32),
            ((heads * tokens, width), BF),
            (own.shape, BF),
        ],
        [((tokens, tokens), F32)],
        4 * tokens * heads * tokens * width,
        8,
    )


def run_near_forward(stacked, scores, tops, near):
    tokens = near[0].shape[1]
    all_rows, width = stacked.shape
    keys = (NEAR + 1) * tokens
    return call(
        functools.partial(near_forward, all_rows // tokens),
        "near_forward",
        (stacked, scores, tops, *near),
        [((keys, all_rows), BF), ((tokens, all_rows // tokens * width), F32), ((16, all_rows), F32)],
        [((keys, width), BF)] * 2 + [((NEAR * tokens, tokens), F32)] * (1 + GROUP),
        4 * keys * all_rows * width,
        16,
    )


def run_far(stacked, out_grad, near_out, stats, own, far):
    tokens = out_grad.shape[0]
    all_rows, width = stacked.shape
    keys = FAR * tokens
    return call(
        functools.partial(far_both, all_rows // tokens),
        "far_both",
        (stacked, out_grad, near_out, stats, own, far),
        [
            (out_grad.shape, BF),
            ((keys, 2 * width), BF),
            (out_grad.shape, F32),
            ((all_rows, width), BF),
            ((8, all_rows), F32),
        ],
        [((keys, width), BF)] * 2
        + [((keys, tokens), F32), ((all_rows, width), BF), ((8, all_rows), F32)]
        + [((keys, all_rows), BF)] * 2
        + [((keys, tokens), F32)] * GROUP,
        10 * keys * all_rows * width,
        FAR_MIB,
    )


def run_near_backward(stacked, near_grad, dots, weights, far_dq, near):
    tokens = far_dq.shape[0]
    all_rows, width = stacked.shape
    keys = (NEAR + 1) * tokens
    return call(
        functools.partial(near_backward, all_rows // tokens),
        "near_backward",
        (stacked, near_grad, dots, weights, far_dq, *near),
        [(far_dq.shape, BF), ((keys, 2 * width), F32)],
        [((keys, width), BF)] * 2 + [((keys, all_rows), BF)],
        8 * keys * all_rows * width,
        16,
    )


def pack_block(k_hbm, v_hbm, seg_hbm, out, seg, *sems):
    tokens, width = k_hbm.shape
    copies = (
        pltpu.make_async_copy(seg_hbm, seg, sems[0]),
        pltpu.make_async_copy(k_hbm, out.at[0:tokens, 0:width], sems[1]),
        pltpu.make_async_copy(v_hbm, out.at[0:tokens, width : 2 * width], sems[2]),
    )
    for copy in copies:
        copy.start()
    copies[0].wait()
    marks = jnp.broadcast_to(seg[...].astype(jnp.float32), (16, tokens))
    out[tokens : tokens + 16, :] = marks.astype(out.dtype)
    copies[1].wait()
    copies[2].wait()


def run_pack(key_rows, value_rows, segment):
    tokens, width = key_rows.shape
    return pl.pallas_call(
        pack_block,
        out_shape=jax.ShapeDtypeStruct((tokens + 16, 2 * width), BF),
        in_specs=[pl.BlockSpec(memory_space=pl.ANY)] * 3,
        out_specs=VM,
        scratch_shapes=[pltpu.VMEM((1, tokens), jnp.int32)] + [pltpu.SemaphoreType.DMA] * 3,
        compiler_params=pltpu.CompilerParams(vmem_limit_bytes=62 << 20),
        name="pack_block",
    )(key_rows, value_rows, segment.reshape(1, tokens))


def add_parts(sums, far, own, *outs):
    tokens = own.shape[0]
    for d in range(FAR):
        out = outs[d - 1] if d else own
        total = sums[rows(d, tokens), :] + far[rows(d, tokens), :].astype(F32)
        out[...] = total.astype(out.dtype)


def run_add(sums, far):
    one = (far.shape[0] // FAR, far.shape[1])
    outs = [(one, F32)] + [(one, BF)] * (FAR - 1)
    return call(add_parts, "add_parts", (sums, far), outs, [], 1, 4)


def on_device(queries, key_rows, value_rows, out_grad, segment):
    tokens, width = key_rows.shape
    own = run_pack(key_rows, value_rows, segment)
    before = [wrapped(own, d) for d in range(1, NEAR + 1)]
    (scores, tops, stacked, own), before = lax.optimization_barrier((run_own(queries, own), before))
    near = [own, *before]
    far = wrapped(jnp.concatenate(near[:FAR], axis=0), 1, "seq")
    weights, near_out, stats = run_near_forward(stacked, scores, tops, near)
    attended, far_part, far_dq, near_grad, dots = run_far(
        stacked, out_grad, near_out, stats, own, far
    )
    far_back = wrapped(far_part, -1, "seq")
    query_grad, sums = run_near_backward(stacked, near_grad, dots, weights, far_dq, near)
    last = wrapped(sums[NEAR * tokens :].astype(BF), -NEAR)
    total, *parts = run_add(sums, far_back)
    for d, part in enumerate(parts):
        total = total + wrapped(part, -d - 1).astype(F32)
    total = total + last.astype(F32)
    return attended, query_grad, total[:, :width], total[:, width:]


def solution(mesh):
    spec = P(AXES, None)
    return jax.shard_map(
        on_device,
        mesh=mesh,
        in_specs=(spec, spec, spec, spec, P(AXES)),
        out_specs=(spec,) * 4,
        check_vma=False,
    )
```

```python
import functools
import math

import jax
import jax.numpy as jnp
from jax import lax
from jax.experimental import pallas as pl
from jax.experimental.pallas import tpu as pltpu
from jax.sharding import PartitionSpec as P

AXES = ("seq", "grp")
NEAR = 3
FAR = 3
NEAR_SIZES = (2, 4)
FAR_SIZES = (0, 1, 3)
GROUP = 8
FAR_MIB = 28
HIDE = -1e30
BF, F32 = jnp.bfloat16, jnp.float32


def wrapped(value, steps, axes=AXES):
    count = lax.axis_size(axes)
    return lax.ppermute(value, axes, [(i, (i + steps) % count) for i in range(count)])


def dot(a, b, over_a, over_b):
    return lax.dot_general(
        a, b, (((over_a,), (over_b,)), ((), ())), preferred_element_type=jnp.float32
    )


def nt(a, b):
    return dot(a, b, 1, 1)


def nn(a, b):
    return dot(a, b, 1, 0)


def tn(a, b):
    return dot(a, b, 0, 0)


def rows(c, size):
    return slice(c * size, (c + 1) * size)


def at(h, size):
    return pl.ds(pl.multiple_of(h * size, size), size)


def marks_of(block, tokens):
    return block[tokens : tokens + 8, :].astype(jnp.float32)


def reached(seg_row, first):
    return jnp.sum(jnp.where(seg_row == first, 1.0, 0.0), axis=1, keepdims=True)


def bias_of(seg_row, row_seg, first, key_at):
    tokens = key_at.shape[0]
    count = reached(seg_row, first)
    shown = (key_at.astype(jnp.float32) >= tokens - count) & (row_seg == first)
    return jnp.where(shown, 0.0, HIDE), jnp.where(count > 0, 1.0, 0.0)


def for_heads(heads, needed, sizes, step, finish=None):
    below = -1
    for size in sizes:

        @pl.when((needed > below) & (needed <= size))
        def _(size=size):
            def group(i, carry):
                step([i * GROUP + k for k in range(GROUP)], size)
                return carry

            lax.fori_loop(0, heads // GROUP, group, 0)
            if finish is not None:
                finish(size)

        below = size


def fold(op, x):
    return op(x.reshape(-1, 8, x.shape[1]), axis=0)


def own_scores(heads, q_ref, own, s_ref, top_ref, qs_ref, held, bias):
    held[...] = own[...]
    tokens = q_ref.shape[0]
    width = q_ref.shape[1] // heads
    scale2 = width**-0.5 * math.log2(math.e)
    own_seg = marks_of(own, tokens)
    key_seg = jnp.transpose(own_seg)[:, 0:1]
    key_at = lax.broadcasted_iota(jnp.int32, (tokens, tokens), 0)
    row_at = lax.broadcasted_iota(jnp.int32, (tokens, tokens), 1)
    shown = (key_seg == own_seg[0:1, :]) & (key_at <= row_at)
    bias[...] = jnp.where(shown, 0.0, HIDE)

    def group(i, carry):
        for k in range(GROUP):
            h = i * GROUP + k
            q = q_ref[:, at(h, width)]
            qs_ref[at(h, tokens), :] = q
            s = nt(own[0:tokens, 0:width], q) * scale2 + bias[...]
            s_ref[:, at(h, tokens)] = s
            top_ref[:, at(h, tokens)] = fold(jnp.max, s)
        return carry

    lax.fori_loop(0, heads // GROUP, group, 0)


def near_forward(heads, q_ref, s_ref, top_ref, *refs):
    blocks = refs[: NEAR + 1]
    e_ref, o_ref, stat_ref, ks, vs, bias, *sc = refs[NEAR + 1 :]
    tokens = q_ref.shape[0] // heads
    width = q_ref.shape[1]
    scale2 = width**-0.5 * math.log2(math.e)
    row_seg = marks_of(blocks[0], tokens)[0:1, :]
    key_at = lax.broadcasted_iota(jnp.int32, (tokens, tokens), 0)
    first = row_seg[:, 0:1]
    reach = jnp.ones((1, 1), jnp.float32)
    for c in range(1, NEAR + 1):
        bias[rows(c - 1, tokens), :], more = bias_of(
            marks_of(blocks[c], tokens)[0:1, :], row_seg, first, key_at
        )
        reach = reach + more
    for c in range(NEAR + 1):
        ks[rows(c, tokens), :] = blocks[c][0:tokens, 0:width]
        vs[rows(c, tokens), :] = blocks[c][0:tokens, width : 2 * width]

    def step(hs, size):
        for k, h in enumerate(hs):
            q = q_ref[at(h, tokens), :]
            top = top_ref[:, at(h, tokens)]
            for c in range(1, size):
                r = rows(c - 1, tokens)
                s = nt(ks[rows(c, tokens), :], q) * scale2 + bias[r, :]
                sc[k][r, :] = s
                top = jnp.maximum(top, fold(jnp.max, s))
            top = jnp.max(top, axis=0, keepdims=True)
            total = jnp.zeros((8, tokens), jnp.float32)
            for c in range(size):
                s = sc[k][rows(c - 1, tokens), :] if c else s_ref[:, at(h, tokens)]
                e = jnp.exp2(s - top)
                total = total + fold(jnp.sum, e)
                e_ref[rows(c, tokens), at(h, tokens)] = e.astype(jnp.bfloat16)
            total = jnp.sum(total, axis=0, keepdims=True)
            stat_ref[0:8, at(h, tokens)] = jnp.broadcast_to(top, (8, tokens))
            stat_ref[8:16, at(h, tokens)] = jnp.broadcast_to(total, (8, tokens))
        seen = slice(0, size * tokens)
        for h in hs:
            o_ref[:, at(h, width)] = tn(e_ref[seen, at(h, tokens)], vs[seen, :])

    for_heads(heads, jnp.sum(reach).astype(jnp.int32), NEAR_SIZES, step)


def far_both(heads, q_ref, g_ref, near_out, stat_ref, own, far, *refs):
    o_ref, part, dq_ref, gn_ref, dots_ref, ks, vs, bias, gf, dt, ex, ds, *sc = refs
    tokens = q_ref.shape[0] // heads
    width = q_ref.shape[1]
    scale = width**-0.5
    scale2 = scale * math.log2(math.e)
    pitch = far.shape[0] // FAR
    row_seg = marks_of(own, tokens)[0:1, :]
    first = row_seg[:, 0:1]
    key_at = lax.broadcasted_iota(jnp.int32, (tokens, tokens), 0)
    reach = jnp.zeros((1, 1), jnp.float32)
    for c in range(FAR):
        seg = far[c * pitch + tokens : c * pitch + tokens + 8, :].astype(jnp.float32)[0:1, :]
        bias[rows(c, tokens), :], more = bias_of(seg, row_seg, first, key_at)
        reach = reach + more
        ks[rows(c, tokens), :] = far[c * pitch : c * pitch + tokens, 0:width]
        vs[rows(c, tokens), :] = far[c * pitch : c * pitch + tokens, width : 2 * width]

    def step(hs, size):
        seen = slice(0, size * tokens)
        tops = []
        for k, h in enumerate(hs):
            q = q_ref[at(h, tokens), :]
            top = jnp.broadcast_to(stat_ref[0:1, at(h, tokens)], (8, tokens))
            for c in range(size):
                r = rows(c, tokens)
                s = nt(ks[r, :], q) * scale2 + bias[r, :]
                sc[k][r, :] = s
                top = jnp.maximum(top, fold(jnp.max, s))
            tops.append(jnp.max(top, axis=0, keepdims=True))
        invs = []
        for k, h in enumerate(hs):
            lanes = at(h, tokens)
            top = tops[k]
            keep = jnp.exp2(stat_ref[0:1, lanes] - top)
            total = jnp.zeros((8, tokens), jnp.float32)
            for c in range(size):
                r = rows(c, tokens)
                e = jnp.exp2(sc[k][r, :] - top)
                total = total + fold(jnp.sum, e)
                ex[r, lanes] = e.astype(jnp.bfloat16)
            total = jnp.sum(total, axis=0, keepdims=True) + stat_ref[8:9, lanes] * keep
            inv = 1.0 / total
            invs.append((inv, inv * keep))
        for k, h in enumerate(hs):
            lanes = at(h, tokens)
            inv, near = invs[k]
            both = jnp.concatenate(
                [jnp.broadcast_to(inv, (8, tokens)), jnp.broadcast_to(near, (8, tokens))], axis=0
            )
            cols = jnp.transpose(both)
            inv_rows, near_rows = cols[:, 0:1], cols[:, 8:9]
            g = g_ref[:, at(h, width)].astype(jnp.float32)
            gf[lanes, :] = (g * inv_rows).astype(jnp.bfloat16)
            gn_ref[lanes, :] = (g * near_rows).astype(jnp.bfloat16)
            out = near_out[:, at(h, width)] * near_rows
            if size:
                out = out + tn(ex[seen, lanes], vs[seen, :]) * inv_rows
            o_ref[:, at(h, width)] = out.astype(o_ref.dtype)
            prod = g * out
            high = prod.astype(jnp.bfloat16)
            low = (prod - high.astype(jnp.float32)).astype(jnp.bfloat16)
            ones = jnp.ones((8, width), jnp.bfloat16)
            dots = nt(ones, high) + nt(ones, low)
            dots_ref[:, lanes] = dots * near
            dt[:, lanes] = dots * inv
        if not size:
            return
        for h in hs:
            lanes = at(h, tokens)
            for c in range(size):
                r = rows(c, tokens)
                d = nt(vs[r, :], gf[lanes, :]) - dt[0:1, lanes]
                ds[r, lanes] = (ex[r, lanes].astype(jnp.float32) * d).astype(jnp.bfloat16)
        for h in hs:
            dq_ref[:, at(h, width)] = tn(ds[seen, at(h, tokens)], ks[seen, :])

    def finish(size):
        seen = slice(0, size * tokens)
        if size:
            values = nn(ex[seen, :], gf[...])
            part[seen, width : 2 * width] = values.astype(part.dtype)
            part[seen, 0:width] = (nn(ds[seen, :], q_ref[...]) * scale).astype(part.dtype)
        else:
            dq_ref[...] = jnp.zeros_like(dq_ref)
        if size < FAR:
            part[size * tokens :, :] = jnp.zeros((part.shape[0] - size * tokens, 2 * width), BF)

    for_heads(heads, jnp.sum(reach).astype(jnp.int32), FAR_SIZES, step, finish)


def near_reach(blocks, tokens):
    row_seg = marks_of(blocks[0], tokens)[0:1, :]
    reach = jnp.ones((1, 1), jnp.float32)
    for block in blocks[1:]:
        count = reached(marks_of(block, tokens)[0:1, :], row_seg[:, 0:1])
        reach = reach + jnp.where(count > 0, 1.0, 0.0)
    return jnp.sum(reach).astype(jnp.int32)


def near_backward(heads, q_ref, gn_ref, dots_ref, e_ref, *refs):
    blocks = refs[: NEAR + 1]
    ds, sums, third, vs = refs[NEAR + 1 :]
    tokens = q_ref.shape[0] // heads
    width = q_ref.shape[1]
    scale = width**-0.5
    for c in range(NEAR):
        vs[rows(c, tokens), :] = blocks[c + 1][0:tokens, width : 2 * width]

    def step(hs, size):
        for h in hs:
            g = gn_ref[at(h, tokens), :]
            lanes = at(h, tokens)
            for c in range(size - 1):
                r = rows(c, tokens)
                d = nt(vs[r, :], g) - dots_ref[0:1, lanes]
                e = e_ref[rows(c + 1, tokens), lanes].astype(jnp.float32)
                ds[r, lanes] = (e * d).astype(jnp.bfloat16)

    def finish(size):
        count = (size - 1) * tokens
        values = nn(e_ref[tokens : tokens + count, :], gn_ref[...])
        keys = nn(ds[0:count, :], q_ref[...]) * scale
        for c in range(NEAR):
            part = third if c == NEAR - 1 else sums.at[rows(c, tokens), :]
            if c < size - 1:
                part[:, 0:width] = keys[rows(c, tokens), :].astype(part.dtype)
                part[:, width : 2 * width] = values[rows(c, tokens), :].astype(part.dtype)
            else:
                part[...] = jnp.zeros(part.shape, part.dtype)

    for_heads(heads, near_reach(blocks, tokens), NEAR_SIZES, step, finish)


def own_backward(heads, q_ref, gn_ref, dots_ref, e_ref, far_dq, ds, *refs):
    blocks = refs[: NEAR + 1]
    dq_ref, own_sum, ks, own_ds = refs[NEAR + 1 :]
    tokens = q_ref.shape[0] // heads
    width = q_ref.shape[1]
    scale = width**-0.5
    for c in range(NEAR):
        ks[rows(c, tokens), :] = blocks[c + 1][0:tokens, 0:width]
    own = blocks[0]

    def step(hs, size):
        seen = slice(0, (size - 1) * tokens)
        for h in hs:
            lanes = at(h, tokens)
            d = nt(own[0:tokens, width : 2 * width], gn_ref[lanes, :]) - dots_ref[0:1, lanes]
            e = e_ref[0:tokens, lanes].astype(jnp.float32)
            own_ds[:, lanes] = (e * d).astype(jnp.bfloat16)
        for h in hs:
            lanes = at(h, width)
            dq = far_dq[:, lanes] + tn(ds[seen, at(h, tokens)], ks[seen, :])
            dq = dq + tn(own_ds[:, at(h, tokens)], own[0:tokens, 0:width])
            dq_ref[:, lanes] = (dq * scale).astype(dq_ref.dtype)

    def finish(size):
        own_sum[:, width : 2 * width] = nn(e_ref[0:tokens, :], gn_ref[...])
        own_sum[:, 0:width] = nn(own_ds[...], q_ref[...]) * scale

    for_heads(heads, near_reach(blocks, tokens), NEAR_SIZES, step, finish)


VM = pl.BlockSpec(memory_space=pltpu.VMEM)


def call(kernel, name, args, outs, scratch, flops, mib):
    return pl.pallas_call(
        kernel,
        out_shape=tuple(jax.ShapeDtypeStruct(*o) for o in outs),
        in_specs=[VM] * len(args),
        out_specs=(VM,) * len(outs),
        scratch_shapes=[pltpu.VMEM(*s) for s in scratch],
        compiler_params=pltpu.CompilerParams(vmem_limit_bytes=mib << 20),
        cost_estimate=pl.CostEstimate(flops=flops, bytes_accessed=1 << 21, transcendentals=0),
        name=name,
    )(*args)


def dims(queries, own):
    tokens = queries.shape[0]
    width = own.shape[1] // 2
    return tokens, width, queries.shape[1] // width


def run_own(queries, own):
    tokens, width, heads = dims(queries, own)
    return call(
        functools.partial(own_scores, heads),
        "own_scores",
        (queries, own),
        [
            ((tokens, heads * tokens), F32),
            ((8, heads * tokens), F32),
            ((heads * tokens, width), BF),
            (own.shape, BF),
        ],
        [((tokens, tokens), F32)],
        4 * tokens * heads * tokens * width,
        8,
    )


def run_near_forward(stacked, scores, tops, near):
    tokens = near[0].shape[1]
    all_rows, width = stacked.shape
    keys = (NEAR + 1) * tokens
    return call(
        functools.partial(near_forward, all_rows // tokens),
        "near_forward",
        (stacked, scores, tops, *near),
        [((keys, all_rows), BF), ((tokens, all_rows // tokens * width), F32), ((16, all_rows), F32)],
        [((keys, width), BF)] * 2 + [((NEAR * tokens, tokens), F32)] * (1 + GROUP),
        4 * keys * all_rows * width,
        16,
    )


def run_far(stacked, out_grad, near_out, stats, own, far):
    tokens = out_grad.shape[0]
    all_rows, width = stacked.shape
    keys = FAR * tokens
    return call(
        functools.partial(far_both, all_rows // tokens),
        "far_both",
        (stacked, out_grad, near_out, stats, own, far),
        [
            (out_grad.shape, BF),
            ((keys, 2 * width), BF),
            (out_grad.shape, F32),
            ((all_rows, width), BF),
            ((8, all_rows), F32),
        ],
        [((keys, width), BF)] * 2
        + [((keys, tokens), F32), ((all_rows, width), BF), ((8, all_rows), F32)]
        + [((keys, all_rows), BF)] * 2
        + [((keys, tokens), F32)] * GROUP,
        10 * keys * all_rows * width,
        FAR_MIB,
    )


def run_near_backward(stacked, near_grad, dots, weights, near):
    tokens = near[0].shape[1]
    all_rows, width = stacked.shape
    keys = NEAR * tokens
    return call(
        functools.partial(near_backward, all_rows // tokens),
        "near_backward",
        (stacked, near_grad, dots, weights, *near),
        [
            ((keys, all_rows), BF),
            ((keys - tokens, 2 * width), F32),
            ((tokens, 2 * width), BF),
        ],
        [((keys, width), BF)],
        6 * keys * all_rows * width,
        12,
    )


def run_own_backward(stacked, near_grad, dots, weights, far_dq, near_ds, near):
    tokens = far_dq.shape[0]
    all_rows, width = stacked.shape
    return call(
        functools.partial(own_backward, all_rows // tokens),
        "own_backward",
        (stacked, near_grad, dots, weights, far_dq, near_ds, *near),
        [(far_dq.shape, BF), ((tokens, 2 * width), F32)],
        [((NEAR * tokens, width), BF), ((tokens, all_rows), BF)],
        14 * tokens * all_rows * width,
        12,
    )


def pack_block(k_hbm, v_hbm, seg_hbm, out, seg, *sems):
    tokens, width = k_hbm.shape
    copies = (
        pltpu.make_async_copy(seg_hbm, seg, sems[0]),
        pltpu.make_async_copy(k_hbm, out.at[0:tokens, 0:width], sems[1]),
        pltpu.make_async_copy(v_hbm, out.at[0:tokens, width : 2 * width], sems[2]),
    )
    for copy in copies:
        copy.start()
    copies[0].wait()
    marks = jnp.broadcast_to(seg[...].astype(jnp.float32), (16, tokens))
    out[tokens : tokens + 16, :] = marks.astype(out.dtype)
    copies[1].wait()
    copies[2].wait()


def run_pack(key_rows, value_rows, segment):
    tokens, width = key_rows.shape
    return pl.pallas_call(
        pack_block,
        out_shape=jax.ShapeDtypeStruct((tokens + 16, 2 * width), BF),
        in_specs=[pl.BlockSpec(memory_space=pl.ANY)] * 3,
        out_specs=VM,
        scratch_shapes=[pltpu.VMEM((1, tokens), jnp.int32)] + [pltpu.SemaphoreType.DMA] * 3,
        compiler_params=pltpu.CompilerParams(vmem_limit_bytes=62 << 20),
        name="pack_block",
    )(key_rows, value_rows, segment.reshape(1, tokens))


def add_parts(sums, far, *outs):
    tokens = outs[0].shape[0]
    for d, out in enumerate(outs):
        total = sums[rows(d, tokens), :] + far[rows(d + 1, tokens), :].astype(F32)
        out[...] = total.astype(out.dtype)


def run_add(sums, far):
    one = (far.shape[0] // FAR, far.shape[1])
    return call(add_parts, "add_parts", (sums, far), [(one, BF)] * (FAR - 1), [], 1, 4)


def on_device(queries, key_rows, value_rows, out_grad, segment):
    tokens, width = key_rows.shape
    own = run_pack(key_rows, value_rows, segment)
    before = [wrapped(own, d) for d in range(1, NEAR + 1)]
    (scores, tops, stacked, own), before = lax.optimization_barrier((run_own(queries, own), before))
    near = [own, *before]
    far = wrapped(jnp.concatenate(near[:FAR], axis=0), 1, "seq")
    weights, near_out, stats = run_near_forward(stacked, scores, tops, near)
    attended, far_part, far_dq, near_grad, dots = run_far(
        stacked, out_grad, near_out, stats, own, far
    )
    far_back = wrapped(far_part, -1, "seq")
    near_ds, sums, third = run_near_backward(stacked, near_grad, dots, weights, near)
    parts = [*run_add(sums, far_back), third]
    query_grad, total = run_own_backward(
        stacked, near_grad, dots, weights, far_dq, near_ds, near
    )
    total = total + far_back[:tokens].astype(F32)
    for d, part in enumerate(parts):
        total = total + wrapped(part, -d - 1).astype(F32)
    return attended, query_grad, total[:, :width], total[:, width:]


def solution(mesh):
    spec = P(AXES, None)
    return jax.shard_map(
        on_device,
        mesh=mesh,
        in_specs=(spec, spec, spec, spec, P(AXES)),
        out_specs=(spec,) * 4,
        check_vma=False,
    )
```

```python
import functools
import math

import jax
import jax.numpy as jnp
from jax import lax
from jax.experimental import pallas as pl
from jax.experimental.pallas import tpu as pltpu
from jax.sharding import PartitionSpec as P

AXES = ("seq", "grp")
NEAR = 3
FAR = 3
NEAR_SIZES = (2, 4)
FAR_SIZES = (0, 1, 3)
GROUP = 8
FAR_MIB = 28
HIDE = -1e30
BF, F32 = jnp.bfloat16, jnp.float32


def wrapped(value, steps, axes=AXES):
    count = lax.axis_size(axes)
    return lax.ppermute(value, axes, [(i, (i + steps) % count) for i in range(count)])


def dot(a, b, over_a, over_b):
    return lax.dot_general(
        a, b, (((over_a,), (over_b,)), ((), ())), preferred_element_type=jnp.float32
    )


def nt(a, b):
    return dot(a, b, 1, 1)


def nn(a, b):
    return dot(a, b, 1, 0)


def tn(a, b):
    return dot(a, b, 0, 0)


def rows(c, size):
    return slice(c * size, (c + 1) * size)


def at(h, size):
    return pl.ds(pl.multiple_of(h * size, size), size)


def marks_of(block, tokens):
    return block[tokens : tokens + 8, :].astype(jnp.float32)


def reached(seg_row, first):
    return jnp.sum(jnp.where(seg_row == first, 1.0, 0.0), axis=1, keepdims=True)


def bias_of(seg_row, row_seg, first, key_at):
    tokens = key_at.shape[0]
    count = reached(seg_row, first)
    shown = (key_at.astype(jnp.float32) >= tokens - count) & (row_seg == first)
    return jnp.where(shown, 0.0, HIDE), jnp.where(count > 0, 1.0, 0.0)


def for_heads(heads, needed, sizes, step, finish=None):
    below = -1
    for size in sizes:

        @pl.when((needed > below) & (needed <= size))
        def _(size=size):
            def group(i, carry):
                step([i * GROUP + k for k in range(GROUP)], size)
                return carry

            lax.fori_loop(0, heads // GROUP, group, 0)
            if finish is not None:
                finish(size)

        below = size


def fold(op, x):
    return op(x.reshape(-1, 8, x.shape[1]), axis=0)


def own_scores(heads, q_ref, own, s_ref, top_ref, qs_ref, held, bias):
    held[...] = own[...]
    tokens = q_ref.shape[0]
    width = q_ref.shape[1] // heads
    scale2 = width**-0.5 * math.log2(math.e)
    own_seg = marks_of(own, tokens)
    key_seg = jnp.transpose(own_seg)[:, 0:1]
    key_at = lax.broadcasted_iota(jnp.int32, (tokens, tokens), 0)
    row_at = lax.broadcasted_iota(jnp.int32, (tokens, tokens), 1)
    shown = (key_seg == own_seg[0:1, :]) & (key_at <= row_at)
    bias[...] = jnp.where(shown, 0.0, HIDE)

    def group(i, carry):
        for k in range(GROUP):
            h = i * GROUP + k
            q = q_ref[:, at(h, width)]
            qs_ref[at(h, tokens), :] = q
            s = nt(own[0:tokens, 0:width], q) * scale2 + bias[...]
            s_ref[:, at(h, tokens)] = s
            top_ref[:, at(h, tokens)] = fold(jnp.max, s)
        return carry

    lax.fori_loop(0, heads // GROUP, group, 0)


def near_forward(heads, q_ref, s_ref, top_ref, *refs):
    blocks = refs[: NEAR + 1]
    e_ref, o_ref, stat_ref, ks, vs, bias, *sc = refs[NEAR + 1 :]
    tokens = q_ref.shape[0] // heads
    width = q_ref.shape[1]
    scale2 = width**-0.5 * math.log2(math.e)
    row_seg = marks_of(blocks[0], tokens)[0:1, :]
    key_at = lax.broadcasted_iota(jnp.int32, (tokens, tokens), 0)
    first = row_seg[:, 0:1]
    reach = jnp.ones((1, 1), jnp.float32)
    for c in range(1, NEAR + 1):
        bias[rows(c - 1, tokens), :], more = bias_of(
            marks_of(blocks[c], tokens)[0:1, :], row_seg, first, key_at
        )
        reach = reach + more
    for c in range(NEAR + 1):
        ks[rows(c, tokens), :] = blocks[c][0:tokens, 0:width]
        vs[rows(c, tokens), :] = blocks[c][0:tokens, width : 2 * width]

    def step(hs, size):
        for k, h in enumerate(hs):
            q = q_ref[at(h, tokens), :]
            top = top_ref[:, at(h, tokens)]
            for c in range(1, size):
                r = rows(c - 1, tokens)
                s = nt(ks[rows(c, tokens), :], q) * scale2 + bias[r, :]
                sc[k][r, :] = s
                top = jnp.maximum(top, fold(jnp.max, s))
            top = jnp.max(top, axis=0, keepdims=True)
            total = jnp.zeros((8, tokens), jnp.float32)
            for c in range(size):
                s = sc[k][rows(c - 1, tokens), :] if c else s_ref[:, at(h, tokens)]
                e = jnp.exp2(s - top)
                total = total + fold(jnp.sum, e)
                e_ref[rows(c, tokens), at(h, tokens)] = e.astype(jnp.bfloat16)
            total = jnp.sum(total, axis=0, keepdims=True)
            stat_ref[0:8, at(h, tokens)] = jnp.broadcast_to(top, (8, tokens))
            stat_ref[8:16, at(h, tokens)] = jnp.broadcast_to(total, (8, tokens))
        seen = slice(0, size * tokens)
        for h in hs:
            o_ref[:, at(h, width)] = tn(e_ref[seen, at(h, tokens)], vs[seen, :])

    for_heads(heads, jnp.sum(reach).astype(jnp.int32), NEAR_SIZES, step)


def far_both(heads, q_ref, g_ref, near_out, stat_ref, own, far, *refs):
    o_ref, *parts = refs[: FAR + 1]
    dq_ref, gn_ref, dots_ref, ks, vs, bias, gf, dt, ex, ds, *sc = refs[FAR + 1 :]
    tokens = q_ref.shape[0] // heads
    width = q_ref.shape[1]
    scale = width**-0.5
    scale2 = scale * math.log2(math.e)
    pitch = far.shape[0] // FAR
    row_seg = marks_of(own, tokens)[0:1, :]
    first = row_seg[:, 0:1]
    key_at = lax.broadcasted_iota(jnp.int32, (tokens, tokens), 0)
    reach = jnp.zeros((1, 1), jnp.float32)
    for c in range(FAR):
        seg = far[c * pitch + tokens : c * pitch + tokens + 8, :].astype(jnp.float32)[0:1, :]
        bias[rows(c, tokens), :], more = bias_of(seg, row_seg, first, key_at)
        reach = reach + more
        ks[rows(c, tokens), :] = far[c * pitch : c * pitch + tokens, 0:width]
        vs[rows(c, tokens), :] = far[c * pitch : c * pitch + tokens, width : 2 * width]

    def step(hs, size):
        seen = slice(0, size * tokens)
        tops = []
        for k, h in enumerate(hs):
            q = q_ref[at(h, tokens), :]
            top = jnp.broadcast_to(stat_ref[0:1, at(h, tokens)], (8, tokens))
            for c in range(size):
                r = rows(c, tokens)
                s = nt(ks[r, :], q) * scale2 + bias[r, :]
                sc[k][r, :] = s
                top = jnp.maximum(top, fold(jnp.max, s))
            tops.append(jnp.max(top, axis=0, keepdims=True))
        invs = []
        for k, h in enumerate(hs):
            lanes = at(h, tokens)
            top = tops[k]
            keep = jnp.exp2(stat_ref[0:1, lanes] - top)
            total = jnp.zeros((8, tokens), jnp.float32)
            for c in range(size):
                r = rows(c, tokens)
                e = jnp.exp2(sc[k][r, :] - top)
                total = total + fold(jnp.sum, e)
                ex[r, lanes] = e.astype(jnp.bfloat16)
            total = jnp.sum(total, axis=0, keepdims=True) + stat_ref[8:9, lanes] * keep
            inv = 1.0 / total
            invs.append((inv, inv * keep))
        for k, h in enumerate(hs):
            lanes = at(h, tokens)
            inv, near = invs[k]
            both = jnp.concatenate(
                [jnp.broadcast_to(inv, (8, tokens)), jnp.broadcast_to(near, (8, tokens))], axis=0
            )
            cols = jnp.transpose(both)
            inv_rows, near_rows = cols[:, 0:1], cols[:, 8:9]
            g = g_ref[:, at(h, width)].astype(jnp.float32)
            gf[lanes, :] = (g * inv_rows).astype(jnp.bfloat16)
            gn_ref[lanes, :] = (g * near_rows).astype(jnp.bfloat16)
            out = near_out[:, at(h, width)] * near_rows
            if size:
                out = out + tn(ex[seen, lanes], vs[seen, :]) * inv_rows
            o_ref[:, at(h, width)] = out.astype(o_ref.dtype)
            prod = g * out
            high = prod.astype(jnp.bfloat16)
            low = (prod - high.astype(jnp.float32)).astype(jnp.bfloat16)
            ones = jnp.ones((8, width), jnp.bfloat16)
            dots = nt(ones, high) + nt(ones, low)
            dots_ref[:, lanes] = dots * near
            dt[:, lanes] = dots * inv
        if not size:
            return
        for h in hs:
            lanes = at(h, tokens)
            for c in range(size):
                r = rows(c, tokens)
                d = nt(vs[r, :], gf[lanes, :]) - dt[0:1, lanes]
                ds[r, lanes] = (ex[r, lanes].astype(jnp.float32) * d).astype(jnp.bfloat16)
        for h in hs:
            dq_ref[:, at(h, width)] = tn(ds[seen, at(h, tokens)], ks[seen, :])

    def finish(size):
        seen = slice(0, size * tokens)
        if size:
            values = nn(ex[seen, :], gf[...]).astype(BF)
            keys = (nn(ds[seen, :], q_ref[...]) * scale).astype(BF)
            for c in range(size):
                parts[c][:, 0:width] = keys[rows(c, tokens), :]
                parts[c][:, width : 2 * width] = values[rows(c, tokens), :]
        else:
            dq_ref[...] = jnp.zeros_like(dq_ref)
        for c in range(size, FAR):
            parts[c][...] = jnp.zeros_like(parts[c])

    for_heads(heads, jnp.sum(reach).astype(jnp.int32), FAR_SIZES, step, finish)


def near_reach(blocks, tokens):
    row_seg = marks_of(blocks[0], tokens)[0:1, :]
    reach = jnp.ones((1, 1), jnp.float32)
    for block in blocks[1:]:
        count = reached(marks_of(block, tokens)[0:1, :], row_seg[:, 0:1])
        reach = reach + jnp.where(count > 0, 1.0, 0.0)
    return jnp.sum(reach).astype(jnp.int32)


def near_backward(heads, q_ref, gn_ref, dots_ref, e_ref, *refs):
    blocks = refs[: NEAR + 1]
    ds, *parts, vs = refs[NEAR + 1 :]
    tokens = q_ref.shape[0] // heads
    width = q_ref.shape[1]
    scale = width**-0.5
    for c in range(NEAR):
        vs[rows(c, tokens), :] = blocks[c + 1][0:tokens, width : 2 * width]

    def step(hs, size):
        for h in hs:
            g = gn_ref[at(h, tokens), :]
            lanes = at(h, tokens)
            for c in range(size - 1):
                r = rows(c, tokens)
                d = nt(vs[r, :], g) - dots_ref[0:1, lanes]
                e = e_ref[rows(c + 1, tokens), lanes].astype(jnp.float32)
                ds[r, lanes] = (e * d).astype(jnp.bfloat16)

    def finish(size):
        count = (size - 1) * tokens
        values = nn(e_ref[tokens : tokens + count, :], gn_ref[...])
        keys = nn(ds[0:count, :], q_ref[...]) * scale
        for c in range(NEAR):
            part = parts[c]
            if c < size - 1:
                part[:, 0:width] = keys[rows(c, tokens), :].astype(part.dtype)
                part[:, width : 2 * width] = values[rows(c, tokens), :].astype(part.dtype)
            else:
                part[...] = jnp.zeros(part.shape, part.dtype)

    for_heads(heads, near_reach(blocks, tokens), NEAR_SIZES, step, finish)


def own_backward(heads, q_ref, gn_ref, dots_ref, e_ref, far_dq, ds, *refs):
    blocks = refs[: NEAR + 1]
    dq_ref, own_sum, ks, own_ds = refs[NEAR + 1 :]
    tokens = q_ref.shape[0] // heads
    width = q_ref.shape[1]
    scale = width**-0.5
    for c in range(NEAR):
        ks[rows(c, tokens), :] = blocks[c + 1][0:tokens, 0:width]
    own = blocks[0]

    def step(hs, size):
        seen = slice(0, (size - 1) * tokens)
        for h in hs:
            lanes = at(h, tokens)
            d = nt(own[0:tokens, width : 2 * width], gn_ref[lanes, :]) - dots_ref[0:1, lanes]
            e = e_ref[0:tokens, lanes].astype(jnp.float32)
            own_ds[:, lanes] = (e * d).astype(jnp.bfloat16)
        for h in hs:
            lanes = at(h, width)
            dq = far_dq[:, lanes] + tn(ds[seen, at(h, tokens)], ks[seen, :])
            dq = dq + tn(own_ds[:, at(h, tokens)], own[0:tokens, 0:width])
            dq_ref[:, lanes] = (dq * scale).astype(dq_ref.dtype)

    def finish(size):
        own_sum[:, width : 2 * width] = nn(e_ref[0:tokens, :], gn_ref[...])
        own_sum[:, 0:width] = nn(own_ds[...], q_ref[...]) * scale

    for_heads(heads, near_reach(blocks, tokens), NEAR_SIZES, step, finish)


VM = pl.BlockSpec(memory_space=pltpu.VMEM)


def call(kernel, name, args, outs, scratch, flops, mib):
    return pl.pallas_call(
        kernel,
        out_shape=tuple(jax.ShapeDtypeStruct(*o) for o in outs),
        in_specs=[VM] * len(args),
        out_specs=(VM,) * len(outs),
        scratch_shapes=[pltpu.VMEM(*s) for s in scratch],
        compiler_params=pltpu.CompilerParams(vmem_limit_bytes=mib << 20),
        cost_estimate=pl.CostEstimate(flops=flops, bytes_accessed=1 << 21, transcendentals=0),
        name=name,
    )(*args)


def dims(queries, own):
    tokens = queries.shape[0]
    width = own.shape[1] // 2
    return tokens, width, queries.shape[1] // width


def run_own(queries, own):
    tokens, width, heads = dims(queries, own)
    return call(
        functools.partial(own_scores, heads),
        "own_scores",
        (queries, own),
        [
            ((tokens, heads * tokens), F32),
            ((8, heads * tokens), F32),
            ((heads * tokens, width), BF),
            (own.shape, BF),
        ],
        [((tokens, tokens), F32)],
        4 * tokens * heads * tokens * width,
        8,
    )


def run_near_forward(stacked, scores, tops, near):
    tokens = near[0].shape[1]
    all_rows, width = stacked.shape
    keys = (NEAR + 1) * tokens
    return call(
        functools.partial(near_forward, all_rows // tokens),
        "near_forward",
        (stacked, scores, tops, *near),
        [((keys, all_rows), BF), ((tokens, all_rows // tokens * width), F32), ((16, all_rows), F32)],
        [((keys, width), BF)] * 2 + [((NEAR * tokens, tokens), F32)] * (1 + GROUP),
        4 * keys * all_rows * width,
        16,
    )


def run_far(stacked, out_grad, near_out, stats, own, far):
    tokens = out_grad.shape[0]
    all_rows, width = stacked.shape
    keys = FAR * tokens
    return call(
        functools.partial(far_both, all_rows // tokens),
        "far_both",
        (stacked, out_grad, near_out, stats, own, far),
        [
            (out_grad.shape, BF),
            *[((tokens, 2 * width), BF)] * FAR,
            (out_grad.shape, F32),
            ((all_rows, width), BF),
            ((8, all_rows), F32),
        ],
        [((keys, width), BF)] * 2
        + [((keys, tokens), F32), ((all_rows, width), BF), ((8, all_rows), F32)]
        + [((keys, all_rows), BF)] * 2
        + [((keys, tokens), F32)] * GROUP,
        10 * keys * all_rows * width,
        FAR_MIB,
    )


def run_near_backward(stacked, near_grad, dots, weights, near):
    tokens = near[0].shape[1]
    all_rows, width = stacked.shape
    keys = NEAR * tokens
    return call(
        functools.partial(near_backward, all_rows // tokens),
        "near_backward",
        (stacked, near_grad, dots, weights, *near),
        [((keys, all_rows), BF)] + [((tokens, 2 * width), BF)] * NEAR,
        [((keys, width), BF)],
        6 * keys * all_rows * width,
        12,
    )


def run_own_backward(stacked, near_grad, dots, weights, far_dq, near_ds, near):
    tokens = far_dq.shape[0]
    all_rows, width = stacked.shape
    return call(
        functools.partial(own_backward, all_rows // tokens),
        "own_backward",
        (stacked, near_grad, dots, weights, far_dq, near_ds, *near),
        [(far_dq.shape, BF), ((tokens, 2 * width), F32)],
        [((NEAR * tokens, width), BF), ((tokens, all_rows), BF)],
        14 * tokens * all_rows * width,
        12,
    )


def pack_block(k_hbm, v_hbm, seg_hbm, out, seg, *sems):
    tokens, width = k_hbm.shape
    copies = (
        pltpu.make_async_copy(seg_hbm, seg, sems[0]),
        pltpu.make_async_copy(k_hbm, out.at[0:tokens, 0:width], sems[1]),
        pltpu.make_async_copy(v_hbm, out.at[0:tokens, width : 2 * width], sems[2]),
    )
    for copy in copies:
        copy.start()
    copies[0].wait()
    marks = jnp.broadcast_to(seg[...].astype(jnp.float32), (16, tokens))
    out[tokens : tokens + 16, :] = marks.astype(out.dtype)
    copies[1].wait()
    copies[2].wait()


def run_pack(key_rows, value_rows, segment):
    tokens, width = key_rows.shape
    return pl.pallas_call(
        pack_block,
        out_shape=jax.ShapeDtypeStruct((tokens + 16, 2 * width), BF),
        in_specs=[pl.BlockSpec(memory_space=pl.ANY)] * 3,
        out_specs=VM,
        scratch_shapes=[pltpu.VMEM((1, tokens), jnp.int32)] + [pltpu.SemaphoreType.DMA] * 3,
        compiler_params=pltpu.CompilerParams(vmem_limit_bytes=62 << 20),
        name="pack_block",
    )(key_rows, value_rows, segment.reshape(1, tokens))


def on_device(queries, key_rows, value_rows, out_grad, segment):
    tokens, width = key_rows.shape
    own = run_pack(key_rows, value_rows, segment)
    before = [wrapped(own, d) for d in range(1, NEAR + 1)]
    (scores, tops, stacked, own), before = lax.optimization_barrier((run_own(queries, own), before))
    near = [own, *before]
    far = wrapped(jnp.concatenate(near[:FAR], axis=0), 1, "seq")
    weights, near_out, stats = run_near_forward(stacked, scores, tops, near)
    attended, *far_parts, far_dq, near_grad, dots = run_far(
        stacked, out_grad, near_out, stats, own, far
    )
    near_ds, *near_parts = run_near_backward(stacked, near_grad, dots, weights, near)
    query_grad, total = run_own_backward(
        stacked, near_grad, dots, weights, far_dq, near_ds, near
    )
    for d, part in enumerate(near_parts + far_parts):
        total = total + wrapped(part, -d - 1).astype(F32)
    return attended, query_grad, total[:, :width], total[:, width:]


def solution(mesh):
    spec = P(AXES, None)
    return jax.shard_map(
        on_device,
        mesh=mesh,
        in_specs=(spec, spec, spec, spec, P(AXES)),
        out_specs=(spec,) * 4,
        check_vma=False,
    )
```
